128 devices in a mesh: tile: 16 (over y, x), depth: 8 (over z, core).
Axes of the slice: x: 4, y: 4, z: 4, core: 2. Of those that a mesh axis runs over, the one named last changes fastest.
Arguments:
- velocity: bfloat16 [3, 128, 1024, 1024], P(None, 'depth', 'tile'), may hold values from -7.5 to 7.5
- palette: float32 [4, 32], replicated, may hold values from 0.02 to 1
- bin_table: int32 [17], replicated, may hold values from 0 to 31
- hot_ids: int32 [16, 4], P('tile'), may hold values from 0 to 127
- repeats: int32 [16, 4], P('tile'), may hold values from 1 to 3
Outputs:
- image_rgb: float32 [3, 1024, 1024], P(None, 'tile', 'depth')
- image_transmit: float32 [1024, 1024], P('tile', 'depth')
- inset_rgb: float32 [16, 4, 3, 64, 1024], P('tile', None, None, None, 'depth')
- inset_transmit: float32 [16, 4, 64, 1024], P('tile', None, None, 'depth')
The draws below stay inside these ranges and needn't reach their ends.
Inputs may be any that keep to these rules, and one draw needn't show every extreme that they name: `hot_ids`: brick ids, tile times 8 plus depth slab.
All inputs are finite; a program needn't handle non-finite values.
Results may differ from the reference program's by a relative error of at most 0.005.
Values may be sent and summed in bfloat16 or wider, within the bound.
A program may use at most 256 MiB of HBM per device.

```python
import math
import jax
import jax.numpy as jnp
import numpy as np
from jax import lax

CX = 64
CZ = 16
NY = 1024
HOT = 4
KNOTS = 17
PAL = 32
MAXREP = 3
NX = 1024
NZ = 128
BRICKS = 128
N_TILE = 16
N_DEPTH = 8


def draw_velocity(key, part):
    key = jax.random.fold_in(key, 11)
    noise_key, amp_key, phase_key = jax.random.split(key, 3)
    depth_pos = jnp.arange(NZ, dtype=jnp.float32)[:, None, None]
    first_pos = jnp.arange(NX, dtype=jnp.float32)[None, :, None]
    second_pos = jnp.arange(NY, dtype=jnp.float32)[None, None, :]
    angle = math.pi / CZ * depth_pos + math.pi / CX * first_pos + 4.0 * math.pi / NY * second_pos
    noise = jnp.clip(jax.random.normal(noise_key, (3, NZ, NX, NY), jnp.float32), -3.5, 3.5)
    amps = jax.random.uniform(amp_key, (3,), jnp.float32, 2.5, 3.5)
    phases = jax.random.uniform(phase_key, (3,), jnp.float32, -math.pi, math.pi)
    wave = amps[:, None, None, None] * jnp.sin(angle[None] + phases[:, None, None, None])
    return (noise + wave).astype(jnp.bfloat16)


def plant(array, rng, low, top_value):
    longest = array.shape.index(max(array.shape))
    spots = []
    for shift in (0, 1):
        where = [jax.random.randint(jax.random.fold_in(rng, axis), (), 0, length) for axis, length in enumerate(array.shape)]
        where[longest] = (where[longest] + shift) % array.shape[longest]
        spots.append(tuple(where))
    return array.at[spots[0]].set(low).at[spots[1]].set(top_value)


def rank_bounds(number_of, slope):
    loads = [(1 << 20) // math.isqrt(rank ** slope) + 1 for rank in range(1, number_of + 1)]
    width = 1 + sum(loads) // (1 << 30)
    return np.cumsum(np.array([max(1, weight // width) for weight in loads]))


def ranked(own_key, extent, count, lean):
    grid = rank_bounds(count, lean)
    ticket = jax.random.randint(jax.random.fold_in(own_key, 1), extent, 0, int(grid[count - 1]))
    rank = jnp.searchsorted(jnp.asarray(grid, jnp.int32), ticket, side="right")
    return jax.random.permutation(jax.random.fold_in(own_key, 2), count)[rank].astype(jnp.int32)


def setup_inputs(seed: int = 0) -> dict:
    seeds = jax.random.split(jax.random.key(seed), 6)
    velocity = draw_velocity(jax.random.fold_in(seeds[5], 71), 0)
    palette = jnp.clip(jax.random.uniform(seeds[1], (4, PAL), jnp.float32, 0.02, 1.0), 0.02, 1.0)
    bin_table = plant(jax.random.randint(seeds[2], (KNOTS,), 0, PAL), jax.random.fold_in(seeds[2], 1), 0, PAL - 1).astype(jnp.int32)
    hot_ids = plant(ranked(seeds[3], (N_TILE, HOT), BRICKS, 2), jax.random.fold_in(seeds[3], 3), 0, BRICKS - 1).astype(jnp.int32)
    repeats = plant(jax.random.randint(seeds[4], (N_TILE, HOT), 1, MAXREP + 1), jax.random.fold_in(seeds[4], 1), 1, MAXREP).astype(jnp.int32)
    return {"velocity": velocity, "palette": palette, "bin_table": bin_table, "hot_ids": hot_ids, "repeats": repeats}


COEF_ONE = 0.75
COEF_TWO = -0.15
COEF_THREE = 1.0 / 60.0


def diff_roll(field, axis):
    first = jnp.roll(field, -1, axis) - jnp.roll(field, 1, axis)
    second = jnp.roll(field, -2, axis) - jnp.roll(field, 2, axis)
    third = jnp.roll(field, -3, axis) - jnp.roll(field, 3, axis)
    return COEF_ONE * first + COEF_TWO * second + COEF_THREE * third


def diff_pad(field, axis, count):
    def piece(offset):
        return lax.slice_in_dim(field, 3 + offset, 3 + offset + count, axis=axis)
    first = piece(1) - piece(-1)
    second = piece(2) - piece(-2)
    third = piece(3) - piece(-3)
    return COEF_ONE * first + COEF_TWO * second + COEF_THREE * third


def q_value(grads):
    total = grads[0][0] * grads[0][0] + grads[1][1] * grads[1][1] + grads[2][2] * grads[2][2]
    cross = grads[0][1] * grads[1][0] + grads[0][2] * grads[2][0] + grads[1][2] * grads[2][1]
    return -0.5 * (total + 2.0 * cross)


def shade(qfield, knot_vals):
    position = (jnp.tanh(qfield) + 1.0) * (0.5 * (KNOTS - 1))
    result = jnp.zeros((4,) + qfield.shape, jnp.float32)
    for knot in range(KNOTS):
        weight = jnp.maximum(0.0, 1.0 - jnp.abs(position - knot))
        result = result + knot_vals[:, knot][:, None, None, None] * weight[None]
    return result


def render(rgba, depth_total):
    tau = rgba[3] * (4.0 / depth_total)
    cum = jnp.cumsum(tau, axis=0)
    weight = (1.0 - jnp.exp(-tau)) * jnp.exp(-(cum - tau))
    colour = jnp.sum(rgba[:3] * weight[None], axis=1)
    return colour, jnp.exp(-cum[-1])


def over(front, back):
    return jnp.concatenate([front[:3] + front[3:4] * back[:3], front[3:4] * back[3:4]], axis=0)


def repeat_fold(image, count):
    colour = image[:3]
    trans = image[3]
    acc = jnp.zeros_like(colour)
    power = jnp.ones_like(trans)
    for turn in range(MAXREP):
        live = turn < count
        acc = acc + jnp.where(live, power[None] * colour, 0.0)
        power = jnp.where(live, power * trans, power)
    return acc, power


def reference(velocity, palette, bin_table, hot_ids, repeats):
    knot_vals = jnp.take(palette, bin_table, axis=1)
    block = 4

    def slab(index):
        def step(carry, inner):
            colour, trans = carry
            start = index * CZ + inner * block
            rows = (start - 3 + jnp.arange(block + 6, dtype=jnp.int32)) % NZ
            window = jnp.take(velocity, rows.astype(jnp.int32), axis=1).astype(jnp.float32)
            grads = []
            for comp in range(3):
                core = window[comp, 3:3 + block]
                grads.append([diff_pad(window[comp], 0, block), diff_roll(core, 1), diff_roll(core, 2)])
            part_colour, part_trans = render(shade(q_value(grads), knot_vals), NZ)
            return (colour + trans[None] * part_colour, trans * part_trans), None
        init = (jnp.zeros((3, NX, NY), jnp.float32), jnp.ones((NX, NY), jnp.float32))
        (colour, trans), _ = lax.scan(step, init, jnp.arange(CZ // block, dtype=jnp.int32))
        return jnp.concatenate([colour, trans[None]], axis=0)

    images = lax.map(slab, jnp.arange(N_DEPTH, dtype=jnp.int32))

    def fold_step(carry, image):
        return over(carry, image), None
    start_image = jnp.concatenate([jnp.zeros((3, NX, NY), jnp.float32), jnp.ones((1, NX, NY), jnp.float32)], axis=0)
    once, _ = lax.scan(fold_step, start_image, images)
    twice = over(once, once)

    stored = lax.optimization_barrier(images.astype(jnp.bfloat16)).astype(jnp.float32)

    def pick(brick):
        tile_no = brick // N_DEPTH
        slab_no = brick % N_DEPTH
        zero = jnp.zeros((), jnp.int32)
        starts = (slab_no.astype(jnp.int32), zero, (tile_no * CX).astype(jnp.int32), zero)
        return lax.dynamic_slice(stored, starts, (1, 4, CX, NY))[0]

    chosen = jax.vmap(pick)(hot_ids.reshape(-1))
    inset_colour, inset_trans = jax.vmap(repeat_fold)(chosen, repeats.reshape(-1))
    inset_rgb = inset_colour.reshape(N_TILE, HOT, 3, CX, NY)
    inset_transmit = inset_trans.reshape(N_TILE, HOT, CX, NY)
    return twice[:3], twice[3], inset_rgb, inset_transmit
```

```python
import functools
import math

import jax
import jax.numpy as jnp
import ml_dtypes
import numpy as np
from jax import lax
from jax.experimental import pallas as pl
from jax.experimental.pallas import tpu as pltpu
from jax.sharding import PartitionSpec as P

KNOTS = 17
MAXREP = 3
STENCIL = ((1, 45.0), (2, -9.0), (3, 1.0))
TAPS = tuple((k, c) for k, c in STENCIL) + tuple((-k, -c) for k, c in STENCIL)
Q_SCALE = -0.5 / 3600.0
BF = jnp.bfloat16
F32 = jnp.float32
ROWS = 16
WIDE = 256
AXIS = 4


def depth_matrix(cells):
    m = np.zeros((cells * ROWS, (cells + 6) * ROWS), np.float32)
    for z in range(cells):
        for r in range(ROWS):
            for k, c in TAPS:
                m[z * ROWS + r, (z + 3 + k) * ROWS + r] = c
    return m


def first_matrix(tiles):
    m = np.zeros((tiles, 4 * ROWS, 13 * ROWS), np.float32)
    for t in range(tiles):
        for p in range(4):
            for r in range(ROWS):
                for k, c in TAPS:
                    g = r + k
                    if 0 <= g < ROWS:
                        col = 4 * ROWS + p * ROWS + g
                    elif g < 0:
                        col = p * ROWS + ROWS + g if t > 0 else 12 * ROWS + 3 * p + 3 + g
                    else:
                        col = 8 * ROWS + p * ROWS + g - ROWS if t < tiles - 1 else 12 * ROWS + 3 * p + g - ROWS
                    m[t, p * ROWS + r, col] = c
    return m


def second_matrix():
    m = np.zeros((2 * WIDE, WIDE), np.float32)
    for l in range(WIDE):
        for k, c in TAPS:
            m[128 + l + k, l] = c
    return m


def pack_matrix():
    m = np.zeros((2, ROWS, 4 * ROWS), np.float32)
    for p in range(4):
        for r in range(3):
            m[0, 3 * p + r, p * ROWS + r] = 1.0
            m[1, 3 * p + r, p * ROWS + ROWS - 3 + r] = 1.0
    return m


def render_kernel(
    sizes,
    vel, palette, bins, hot_smem, hot_vmem, reps, dz_ref, dx_ref, band_ref, pack_ref,
    img_rgb, img_t, ins_rgb, ins_t,
    vz, xsend, xh, grad, tab, packets, arrive, held, shelf, picked, landed, hot_all, hot_here,
    own_sem, zs_sem, zr_sem, xs_sem, xr_sem, hs_sem, hr_sem, hl_sem,
    as_sem, ar_sem, s1_sem, r1_sem, s2_sem, r2_sem,
):
    cells, width, length, n_depth, n_tile, hot = sizes
    tiles = width // ROWS
    blocks = length // WIDE
    tile = lax.axis_index("tile")
    me = lax.axis_index("depth")
    pos = (tile // AXIS, lax.rem(tile, AXIS))

    def peer(axis, i):
        place = lax.rem(pos[axis] + i, AXIS)
        return place, (place * AXIS + pos[1] if axis == 0 else pos[0] * AXIS + place)

    tile_up = lax.rem(tile + 1, n_tile)
    tile_down = lax.rem(tile + n_tile - 1, n_tile)
    depth_up = lax.rem(me + 1, n_depth)
    depth_down = lax.rem(me + n_depth - 1, n_depth)

    def own_copy(t):
        rows = pl.ds(t * ROWS, ROWS)
        return pltpu.make_async_copy(
            vel.at[:, :, rows, :], vz.at[:, pl.ds(3, cells), rows, :], own_sem.at[t]
        )

    for t in (0, 3, 1, 2):
        own_copy(t).start()

    barrier = pltpu.get_barrier_semaphore()
    for t in (tile_up, tile_down):
        pl.semaphore_signal(barrier, inc=1, device_id={"tile": t})
    for i in range(1, n_depth):
        pl.semaphore_signal(barrier, inc=1, device_id={"depth": lax.rem(me + i, n_depth)})
    for axis in (0, 1):
        for i in range(1, AXIS):
            pl.semaphore_signal(barrier, inc=1, device_id={"tile": peer(axis, i)[1]})
    pl.semaphore_wait(barrier, 2 + n_depth - 1 + 2 * (AXIS - 1))

    def z_copy(s, up):
        rows = pl.ds(lax.rem(s + 1, tiles) * ROWS, ROWS)
        source, target = (cells - 3, 0) if up else (0, cells + 3)
        return pltpu.make_async_remote_copy(
            src_ref=vel.at[:, pl.ds(source, 3), rows, :],
            dst_ref=vz.at[:, pl.ds(target, 3), rows, :],
            send_sem=zs_sem.at[s, int(up)],
            recv_sem=zr_sem.at[s, int(up)],
            device_id={"depth": depth_up if up else depth_down},
        )

    for s in range(tiles):
        for up in (True, False):
            z_copy(s, up).start()

    def hot_copy(axis, i):
        return pltpu.make_async_remote_copy(
            src_ref=hot_vmem,
            dst_ref=hot_all.at[axis, pos[axis]],
            send_sem=hs_sem.at[axis, i - 1],
            recv_sem=hr_sem.at[axis, pos[axis]],
            device_id={"tile": peer(axis, i)[1]},
        )

    def hot_arrival(axis, i):
        place, to = peer(axis, i)
        return pltpu.make_async_remote_copy(
            src_ref=hot_vmem, dst_ref=hot_all.at[axis, place],
            send_sem=hs_sem.at[axis, i - 1], recv_sem=hr_sem.at[axis, place],
            device_id={"tile": to},
        )

    for axis in (0, 1):
        for i in range(1, AXIS):
            hot_copy(axis, i).start()
        hot_all[axis, pos[axis]] = hot_vmem[...]

    own_copy(0).wait()
    own_copy(3).wait()
    for side in (0, 1):
        rows = pl.ds((tiles - 1) * ROWS * side, ROWS)

        def pack(g, carry, side=side, rows=rows):
            planes = vz[g // (cells // 4), pl.ds(3 + 4 * lax.rem(g, cells // 4), 4), rows, :]
            xsend[side, g] = jnp.dot(
                pack_ref[side], planes.reshape(4 * ROWS, length), preferred_element_type=F32
            ).astype(BF)
            return carry

        lax.fori_loop(0, 3 * cells // 4, pack, 0)

    def x_copy(side):
        return pltpu.make_async_remote_copy(
            src_ref=xsend.at[side],
            dst_ref=xh.at[1 - side],
            send_sem=xs_sem.at[side],
            recv_sem=xr_sem.at[side],
            device_id={"tile": tile_up if side else tile_down},
        )

    x_copy(0).start()
    x_copy(1).start()
    xh[2] = jnp.zeros(xh.shape[1:], BF)

    lane = lax.broadcasted_iota(jnp.int32, (8, 128), 1)
    for c in range(4):
        scale = -4.0 / (cells * n_depth) * math.log2(math.e) if c == 3 else 1.0
        values = [palette[c, bins[k]] * scale for k in range(KNOTS)]
        base = jnp.full((8, 128), values[KNOTS - 1], F32)
        slope = jnp.zeros((8, 128), F32)
        for k in range(KNOTS - 1):
            base = jnp.where(lane == k, values[k], base)
            slope = jnp.where(lane == k, values[k + 1] - values[k], slope)
        tab[2 * c] = base
        tab[2 * c + 1] = slope

    own_copy(1).wait()
    own_copy(2).wait()

    def a2a_copy(s, to):
        return pltpu.make_async_remote_copy(
            src_ref=packets.at[s, to],
            dst_ref=arrive.at[s, me],
            send_sem=as_sem.at[s, to],
            recv_sem=ar_sem.at[s, me],
            device_id={"depth": to},
        )

    def a2a_arrival(s, source):
        return pltpu.make_async_remote_copy(
            src_ref=packets.at[s, source],
            dst_ref=arrive.at[s, source],
            send_sem=as_sem.at[s, source],
            recv_sem=ar_sem.at[s, source],
            device_id={"depth": source},
        )

    def a2a_own(s):
        return pltpu.make_async_copy(packets.at[s, me], arrive.at[s, me], ar_sem.at[s, me])

    def block_step(b, s):
        t = lax.rem(s + 1, tiles)
        row = pl.multiple_of(t * ROWS, ROWS)
        above = pl.multiple_of(jnp.maximum(t - 1, 0) * ROWS, ROWS)
        below = pl.multiple_of(jnp.minimum(t + 1, tiles - 1) * ROWS, ROWS)
        side = jnp.where(t == 0, 0, jnp.where(t == tiles - 1, 1, 2))
        col = pl.multiple_of(b * WIDE, WIDE)
        before = pl.multiple_of(lax.rem(col + length - 128, length), 128)
        after = pl.multiple_of(lax.rem(col + WIDE, length), 128)
        cols = pl.ds(col, WIDE)
        size = cells * ROWS
        for comp in range(3):
            column = vz[comp, :, pl.ds(row, ROWS), cols].reshape((cells + 6) * ROWS, WIDE)
            grad[3 * comp] = jnp.dot(dz_ref[...], column, preferred_element_type=F32)
            for quad in range(cells // 4):
                zs = pl.ds(3 + 4 * quad, 4)
                parts = [
                    vz[comp, zs, pl.ds(r, ROWS), cols].reshape(4 * ROWS, WIDE)
                    for r in (above, row, below)
                ] + [xh[side, comp * (cells // 4) + quad, :, cols]]
                grad[3 * comp + 1, pl.ds(quad * 4 * ROWS, 4 * ROWS)] = jnp.dot(
                    dx_ref[t], jnp.concatenate(parts, axis=0), preferred_element_type=F32
                )
            line = jnp.concatenate(
                [
                    vz[comp, pl.ds(3, cells), pl.ds(row, ROWS), c].reshape(size, -1)
                    for c in (pl.ds(before, 128), cols, pl.ds(after, 128))
                ],
                axis=1,
            )
            grad[3 * comp + 2] = jnp.dot(line, band_ref[...], preferred_element_type=F32)

        for h in range(WIDE // 128):
            to = b * (WIDE // 128) + h
            halves = []
            for r in range(ROWS // 8):
                cum = jnp.zeros((8, 128), F32)
                trans = jnp.ones((8, 128), F32)
                colour = [jnp.zeros((8, 128), F32) for _ in range(3)]
                for z in range(cells):
                    a = [grad[j, pl.ds(z * ROWS + 8 * r, 8), pl.ds(128 * h, 128)] for j in range(9)]
                    q = a[0] * a[0] + a[4] * a[4] + a[8] * a[8]
                    q = q + 2.0 * (a[1] * a[3] + a[2] * a[6] + a[5] * a[7])
                    place = jnp.tanh(q * Q_SCALE) * (0.5 * (KNOTS - 1)) + 0.5 * (KNOTS - 1)
                    index = place.astype(jnp.int32)
                    part = place - index.astype(F32)

                    def look(j, index=index):
                        return jnp.take_along_axis(tab[j], index, axis=1, mode="promise_in_bounds")

                    cum = cum + (look(6) + look(7) * part)
                    behind = jnp.exp2(cum)
                    weight = trans - behind
                    trans = behind
                    colour = [
                        colour[c] + (look(2 * c) + look(2 * c + 1) * part) * weight for c in range(3)
                    ]
                halves.append(colour + [trans])
            for c in range(4):
                full = jnp.concatenate([half[c] for half in halves], axis=0)
                high = full.astype(BF)
                packets[s, to, c] = high
                if c == 3:
                    packets[s, to, 4] = (full - high.astype(F32)).astype(BF)

            @pl.when(to == me)
            def _(to=to):
                a2a_own(s).start()

            @pl.when(to != me)
            def _(to=to):
                a2a_copy(s, to).start()

        return s

    def gather_copy(s, axis, i):
        return pltpu.make_async_remote_copy(
            src_ref=arrive.at[s, :, pl.ds(2 * axis, 2)],
            dst_ref=held.at[axis, s, pos[axis]],
            send_sem=s1_sem.at[s, axis, i - 1],
            recv_sem=r1_sem.at[s, axis, pos[axis]],
            device_id={"tile": peer(axis, i)[1]},
        )

    def gather_arrival(s, axis, i):
        place, to = peer(axis, i)
        return pltpu.make_async_remote_copy(
            src_ref=arrive.at[s, :, pl.ds(2 * axis, 2)],
            dst_ref=held.at[axis, s, place],
            send_sem=s1_sem.at[s, axis, i - 1],
            recv_sem=r1_sem.at[s, axis, place],
            device_id={"tile": to},
        )

    def pick_copy(s, axis, i):
        other = 1 - axis
        place, to = peer(other, i)
        return pltpu.make_async_remote_copy(
            src_ref=picked.at[axis, s, place],
            dst_ref=landed.at[axis, s, pos[other]],
            send_sem=s2_sem.at[s, axis, i - 1],
            recv_sem=r2_sem.at[s, axis, pos[other]],
            device_id={"tile": to},
        )

    def pick_arrival(s, axis, i):
        place, to = peer(1 - axis, i)
        return pltpu.make_async_remote_copy(
            src_ref=picked.at[axis, s, place],
            dst_ref=landed.at[axis, s, place],
            send_sem=s2_sem.at[s, axis, i - 1],
            recv_sem=r2_sem.at[s, axis, place],
            device_id={"tile": to},
        )

    def frame_step(s):
        rows = pl.ds(pl.multiple_of(lax.rem(s + 1, tiles) * ROWS, ROWS), ROWS)
        for i in range(1, n_depth):
            a2a_arrival(s, lax.rem(me + i, n_depth)).wait_recv()
        a2a_own(s).wait()
        for axis in (0, 1):
            for i in range(1, AXIS):
                gather_copy(s, axis, i).start()
        colour = [jnp.zeros((ROWS, 128), F32) for _ in range(3)]
        trans = jnp.ones((ROWS, 128), F32)
        for d in range(n_depth):
            image = [arrive[s, d, c] for c in range(5)]
            for axis in (0, 1):
                for c in (0, 1):
                    held[axis, s, pos[axis], d, c] = image[2 * axis + c]
            colour = [colour[c] + trans * image[c].astype(F32) for c in range(3)]
            trans = trans * (image[3].astype(F32) + image[4].astype(F32))
        for c in range(3):
            img_rgb[c, rows, :] = colour[c] + trans * colour[c]
        img_t[rows, :] = trans * trans

    def pick_step(s):
        @pl.when(s == 0)
        def _():
            for axis in (0, 1):
                for i in range(1, AXIS):
                    hot_arrival(axis, i).wait_recv()
            everything = pltpu.make_async_copy(hot_all, hot_here, hl_sem)
            everything.start()
            everything.wait()

        for axis in (0, 1):
            for i in range(1, AXIS):
                gather_arrival(s, axis, i).wait_recv()
            shelf[axis] = held[axis, s]
            for i in range(AXIS):
                place, _ = peer(1 - axis, i)
                for h in range(hot):
                    brick = hot_here[1 - axis, place, 0, h]
                    its_tile, slab = brick // n_depth, lax.rem(brick, n_depth)
                    its_place = its_tile // AXIS if axis == 0 else lax.rem(its_tile, AXIS)
                    image = shelf[axis, its_place, slab]
                    if i == 0:
                        landed[axis, s, place, h] = image
                    else:
                        picked[axis, s, place, h] = image
                if i > 0:
                    pick_copy(s, axis, i).start()

    def choose(axis, s, h, place):
        image = landed[axis, s, 0, h].astype(F32)
        for i in range(1, AXIS):
            image = jnp.where(place == i, landed[axis, s, i, h].astype(F32), image)
        return image

    def inset_step(s):
        rows = pl.ds(pl.multiple_of(lax.rem(s + 1, tiles) * ROWS, ROWS), ROWS)
        for axis in (0, 1):
            for i in range(1, AXIS):
                pick_arrival(s, axis, i).wait_recv()
        for h in range(hot):
            its_tile = hot_smem[0, h] // n_depth
            first = choose(0, s, h, lax.rem(its_tile, AXIS))
            last = choose(1, s, h, its_tile // AXIS)
            count = reps[0, h]
            trans = last[1]
            two = jnp.where(count >= 2, trans, 0.0)
            three = jnp.where(count >= 3, trans * trans, 0.0)
            total = 1.0 + two + three
            ins_rgb[0, h, 0, rows, :] = first[0] * total
            ins_rgb[0, h, 1, rows, :] = first[1] * total
            ins_rgb[0, h, 2, rows, :] = last[0] * total
            power = jnp.where(count >= 2, trans, 1.0) * trans
            ins_t[0, h, rows, :] = jnp.where(count >= 3, trans, 1.0) * power

    def step(k, carry):
        @pl.when(k < tiles)
        def _():
            z_copy(k, True).wait_recv()
            z_copy(k, False).wait_recv()

            @pl.when(k == tiles - 2)
            def _():
                x_copy(0).wait_recv()

            @pl.when(k == tiles - 1)
            def _():
                x_copy(1).wait_recv()

            lax.fori_loop(0, blocks, block_step, k)

        @pl.when((k >= 1) & (k < tiles + 1))
        def _():
            frame_step(k - 1)

        @pl.when((k >= 2) & (k < tiles + 2))
        def _():
            pick_step(k - 2)

        @pl.when(k >= 3)
        def _():
            inset_step(k - 3)

        return carry

    lax.fori_loop(0, tiles + 3, step, 0)

    for axis in (0, 1):
        for i in range(1, AXIS):
            hot_copy(axis, i).wait_send()
    x_copy(0).wait_send()
    x_copy(1).wait_send()

    def sent(s, carry):
        z_copy(s, True).wait_send()
        z_copy(s, False).wait_send()
        for i in range(1, n_depth):
            a2a_copy(s, lax.rem(me + i, n_depth)).wait_send()
        for axis in (0, 1):
            for i in range(1, AXIS):
                gather_copy(s, axis, i).wait_send()
                pick_copy(s, axis, i).wait_send()
        return carry

    lax.fori_loop(0, tiles, sent, 0)


def body(velocity, palette, bin_table, hot_ids, repeats):
    _, cells, width, length = velocity.shape
    n_depth, n_tile = lax.axis_size("depth"), lax.axis_size("tile")
    hot = hot_ids.shape[1]
    tiles = width // ROWS
    groups = 3 * cells // 4
    vmem, smem = pl.BlockSpec(memory_space=pltpu.VMEM), pl.BlockSpec(memory_space=pltpu.SMEM)
    dma, one = pltpu.SemaphoreType.DMA, pltpu.SemaphoreType.DMA
    constants = [
        jnp.asarray(m.astype(ml_dtypes.bfloat16))
        for m in (depth_matrix(cells), first_matrix(tiles), second_matrix(), pack_matrix())
    ]
    columns = length // n_depth
    return pl.pallas_call(
        functools.partial(render_kernel, (cells, width, length, n_depth, n_tile, hot)),
        out_shape=(
            jax.ShapeDtypeStruct((3, width, columns), F32),
            jax.ShapeDtypeStruct((width, columns), F32),
            jax.ShapeDtypeStruct((1, hot, 3, width, columns), F32),
            jax.ShapeDtypeStruct((1, hot, width, columns), F32),
        ),
        in_specs=[pl.BlockSpec(memory_space=pl.ANY), smem, smem, smem, vmem, smem] + [vmem] * 4,
        out_specs=(vmem, vmem, vmem, vmem),
        scratch_shapes=[
            pltpu.VMEM((3, cells + 6, width, length), BF),
            pltpu.VMEM((2, groups, ROWS, length), BF),
            pltpu.VMEM((3, groups, ROWS, length), BF),
            pltpu.VMEM((9, cells * ROWS, WIDE), F32),
            pltpu.VMEM((8, 8, 128), F32),
            pltpu.VMEM((tiles, n_depth, 5, ROWS, columns), BF),
            pltpu.VMEM((tiles, n_depth, 5, ROWS, columns), BF),
            pltpu.VMEM((2, tiles, AXIS, n_depth, 2, ROWS, columns), BF),
            pltpu.VMEM((2, AXIS, n_depth, 2, ROWS, columns), BF),
            pltpu.VMEM((2, tiles, AXIS, hot, 2, ROWS, columns), BF),
            pltpu.VMEM((2, tiles, AXIS, hot, 2, ROWS, columns), BF),
            pltpu.VMEM((2, AXIS, 1, hot), jnp.int32),
            pltpu.SMEM((2, AXIS, 1, hot), jnp.int32),
            dma((tiles,)),
            dma((tiles, 2)), dma((tiles, 2)),
            dma((2,)), dma((2,)),
            dma((2, AXIS)), dma((2, AXIS)), pltpu.SemaphoreType.DMA,
            dma((tiles, n_depth)), dma((tiles, n_depth)),
            dma((tiles, 2, AXIS)), dma((tiles, 2, AXIS)),
            dma((tiles, 2, AXIS)), dma((tiles, 2, AXIS)),
        ],
        compiler_params=pltpu.CompilerParams(
            collective_id=0, has_side_effects=True, vmem_limit_bytes=48 * 2**20
        ),
        cost_estimate=pl.CostEstimate(
            flops=3 * cells * width * length * 400, bytes_accessed=velocity.size * 2, transcendentals=0
        ),
        name="render",
    )(velocity, palette, bin_table, hot_ids, hot_ids, repeats, *constants)


def solution(mesh):
    placed = (P(None, "depth", "tile", None), P(), P(), P("tile", None), P("tile", None))
    return jax.shard_map(
        body,
        mesh=mesh,
        in_specs=placed,
        out_specs=(
            P(None, "tile", "depth"),
            P("tile", "depth"),
            P("tile", None, None, None, "depth"),
            P("tile", None, None, "depth"),
        ),
        check_vma=False,
    )
```

```python
import functools
import math

import jax
import jax.numpy as jnp
import ml_dtypes
import numpy as np
from jax import lax
from jax.experimental import pallas as pl
from jax.experimental.pallas import tpu as pltpu
from jax.sharding import PartitionSpec as P

KNOTS = 17
MAXREP = 3
STENCIL = ((1, 45.0), (2, -9.0), (3, 1.0))
TAPS = tuple((k, c) for k, c in STENCIL) + tuple((-k, -c) for k, c in STENCIL)
HIGH, LOW = 32760.0, 32767.0
Q_SCALE = -0.5 / 3600.0
BF = jnp.bfloat16
F32 = jnp.float32
ROWS = 16
WIDE = 256
AXIS = 4


def depth_matrix(cells):
    m = np.zeros((cells * ROWS, (cells + 6) * ROWS), np.float32)
    for z in range(cells):
        for r in range(ROWS):
            for k, c in TAPS:
                m[z * ROWS + r, (z + 3 + k) * ROWS + r] = c
    return m


def first_matrix(tiles):
    m = np.zeros((tiles, 4 * ROWS, 13 * ROWS), np.float32)
    for t in range(tiles):
        for p in range(4):
            for r in range(ROWS):
                for k, c in TAPS:
                    g = r + k
                    if 0 <= g < ROWS:
                        col = 4 * ROWS + p * ROWS + g
                    elif g < 0:
                        col = p * ROWS + ROWS + g if t > 0 else 12 * ROWS + 3 * p + 3 + g
                    else:
                        col = 8 * ROWS + p * ROWS + g - ROWS if t < tiles - 1 else 12 * ROWS + 3 * p + g - ROWS
                    m[t, p * ROWS + r, col] = c
    return m


def second_matrix():
    m = np.zeros((2 * WIDE, WIDE), np.float32)
    for l in range(WIDE):
        for k, c in TAPS:
            m[128 + l + k, l] = c
    return m


def pack_matrix():
    m = np.zeros((2, ROWS, 4 * ROWS), np.float32)
    for p in range(4):
        for r in range(3):
            m[0, 3 * p + r, p * ROWS + r] = 1.0
            m[1, 3 * p + r, p * ROWS + ROWS - 3 + r] = 1.0
    return m


def render_kernel(
    sizes,
    vel, palette_in, bins_in, hot_in, reps_in, dz_in, dx_in, band_in, pack_in,
    img_rgb, img_t, ins_rgb, ins_t,
    palette, bins, hot_smem, hot_vmem, reps, dz_ref, dx_ref, band_ref, pack_ref,
    vz, xsend, xh, flat, deep_even, deep_odd, tab, unit, packets, arrive, held, shelf, picked, landed, hot_all, hot_here,
    in_sem, own_sem, zs_sem, zr_sem, xs_sem, xr_sem, hs_sem, hr_sem, hl_sem,
    as_sem, ar_sem, s1_sem, r1_sem, s2_sem, r2_sem,
):
    cells, width, length, n_depth, n_tile, hot = sizes
    tiles = width // ROWS
    blocks = length // WIDE
    tile = lax.axis_index("tile")
    me = lax.axis_index("depth")
    pos = (tile // AXIS, lax.rem(tile, AXIS))

    def peer(axis, i):
        place = lax.rem(pos[axis] + i, AXIS)
        return place, (place * AXIS + pos[1] if axis == 0 else pos[0] * AXIS + place)

    tile_up = lax.rem(tile + 1, n_tile)
    tile_down = lax.rem(tile + n_tile - 1, n_tile)
    depth_up = lax.rem(me + 1, n_depth)
    depth_down = lax.rem(me + n_depth - 1, n_depth)

    small = [
        pltpu.make_async_copy(source, target, in_sem.at[n])
        for n, (source, target) in enumerate(
            (
                (hot_in, hot_vmem), (pack_in, pack_ref), (palette_in, palette), (bins_in, bins),
                (hot_in, hot_smem), (reps_in, reps), (dz_in, dz_ref), (dx_in, dx_ref), (band_in, band_ref),
            )
        )
    ]

    def own_copy(t):
        rows = pl.ds(t * ROWS, ROWS)
        return pltpu.make_async_copy(
            vel.at[:, :, rows, :], vz.at[:, pl.ds(3, cells), rows, :], own_sem.at[t]
        )

    own_copy(0).start()
    own_copy(3).start()
    for copy in small:
        copy.start()
    own_copy(1).start()
    own_copy(2).start()

    barrier = pltpu.get_barrier_semaphore()
    for t in (tile_up, tile_down):
        pl.semaphore_signal(barrier, inc=1, device_id={"tile": t})
    for i in range(1, n_depth):
        pl.semaphore_signal(barrier, inc=1, device_id={"depth": lax.rem(me + i, n_depth)})
    for axis in (0, 1):
        for i in range(1, AXIS):
            pl.semaphore_signal(barrier, inc=1, device_id={"tile": peer(axis, i)[1]})
    pl.semaphore_wait(barrier, 2 + n_depth - 1 + 2 * (AXIS - 1))

    def z_copy(s, up):
        rows = pl.ds(lax.rem(s + 1, tiles) * ROWS, ROWS)
        source, target = (cells - 3, 0) if up else (0, cells + 3)
        return pltpu.make_async_remote_copy(
            src_ref=vel.at[:, pl.ds(source, 3), rows, :],
            dst_ref=vz.at[:, pl.ds(target, 3), rows, :],
            send_sem=zs_sem.at[s, int(up)],
            recv_sem=zr_sem.at[s, int(up)],
            device_id={"depth": depth_up if up else depth_down},
        )

    for s in range(tiles):
        for up in (True, False):
            z_copy(s, up).start()

    def hot_copy(axis, i):
        return pltpu.make_async_remote_copy(
            src_ref=hot_vmem,
            dst_ref=hot_all.at[axis, pos[axis]],
            send_sem=hs_sem.at[axis, i - 1],
            recv_sem=hr_sem.at[axis, pos[axis]],
            device_id={"tile": peer(axis, i)[1]},
        )

    def hot_arrival(axis, i):
        place, to = peer(axis, i)
        return pltpu.make_async_remote_copy(
            src_ref=hot_vmem, dst_ref=hot_all.at[axis, place],
            send_sem=hs_sem.at[axis, i - 1], recv_sem=hr_sem.at[axis, place],
            device_id={"tile": to},
        )

    small[0].wait()
    for axis in (0, 1):
        for i in range(1, AXIS):
            hot_copy(axis, i).start()
        hot_all[axis, pos[axis]] = hot_vmem[...]

    def x_copy(side, comp):
        groups = pl.ds(comp * (cells // 4), cells // 4)
        return pltpu.make_async_remote_copy(
            src_ref=xsend.at[side, groups],
            dst_ref=xh.at[1 - side, groups],
            send_sem=xs_sem.at[side, comp],
            recv_sem=xr_sem.at[side, comp],
            device_id={"tile": tile_up if side else tile_down},
        )

    own_copy(0).wait()
    own_copy(3).wait()
    small[1].wait()

    def pack(comp, carry):
        for side in (0, 1):
            rows = pl.ds((tiles - 1) * ROWS * side, ROWS)
            for quad in range(cells // 4):
                planes = vz[comp, pl.ds(3 + 4 * quad, 4), rows, :]
                xsend[side, comp * (cells // 4) + quad] = jnp.dot(
                    pack_ref[side], planes.reshape(4 * ROWS, length), preferred_element_type=F32
                ).astype(BF)
            x_copy(side, comp).start()
        return carry

    lax.fori_loop(0, 3, pack, 0)
    xh[2] = jnp.zeros(xh.shape[1:], BF)

    for copy in small[2:]:
        copy.wait()
    lane = lax.broadcasted_iota(jnp.int32, (8, 128), 1)
    for c in range(4):
        values = [palette[c, bins[k]] for k in range(KNOTS)]
        base = jnp.full((8, 128), values[KNOTS - 1], F32)
        following = base
        for k in range(KNOTS - 1):
            base = jnp.where(lane == k, values[k], base)
            following = jnp.where(lane == k, values[k + 1], following)
        top = jnp.broadcast_to(jnp.max(base, axis=1, keepdims=True), (8, 128))
        low = jnp.floor((following - base) / top * LOW + 0.5)
        high = jnp.floor(base / top * HIGH - low * (1.0 / 65536.0) + 0.5)
        tab[c] = high.astype(jnp.int32) * 65536 + low.astype(jnp.int32)
        if c == 3:
            unit[c] = top * (-4.0 / (cells * n_depth) * math.log2(math.e) / (HIGH * 65536.0))
        else:
            unit[c] = top * (1.0 / (HIGH * 65536.0))

    own_copy(1).wait()
    own_copy(2).wait()

    def a2a_copy(s, to):
        return pltpu.make_async_remote_copy(
            src_ref=packets.at[s, to],
            dst_ref=arrive.at[s, me],
            send_sem=as_sem.at[s, to],
            recv_sem=ar_sem.at[s, me],
            device_id={"depth": to},
        )

    def a2a_arrival(s, source):
        return pltpu.make_async_remote_copy(
            src_ref=packets.at[s, source],
            dst_ref=arrive.at[s, source],
            send_sem=as_sem.at[s, source],
            recv_sem=ar_sem.at[s, source],
            device_id={"depth": source},
        )

    def a2a_own(s):
        return pltpu.make_async_copy(packets.at[s, me], arrive.at[s, me], ar_sem.at[s, me])

    def first_second(b, s):
        t = lax.rem(s + 1, tiles)
        row = pl.multiple_of(t * ROWS, ROWS)
        above = pl.multiple_of(jnp.maximum(t - 1, 0) * ROWS, ROWS)
        below = pl.multiple_of(jnp.minimum(t + 1, tiles - 1) * ROWS, ROWS)
        side = jnp.where(t == 0, 0, jnp.where(t == tiles - 1, 1, 2))
        col = pl.multiple_of(b * WIDE, WIDE)
        before = pl.multiple_of(lax.rem(col + length - 128, length), 128)
        after = pl.multiple_of(lax.rem(col + WIDE, length), 128)
        cols = pl.ds(col, WIDE)
        for comp in range(3):
            for quad in range(cells // 4):
                zs = pl.ds(3 + 4 * quad, 4)
                parts = [
                    vz[comp, zs, pl.ds(r, ROWS), cols].reshape(4 * ROWS, WIDE)
                    for r in (above, row, below)
                ] + [xh[side, comp * (cells // 4) + quad, :, cols]]
                flat[b, 2 * comp, pl.ds(quad * 4 * ROWS, 4 * ROWS)] = jnp.dot(
                    dx_ref[t], jnp.concatenate(parts, axis=0), preferred_element_type=F32
                )
            line = jnp.concatenate(
                [
                    vz[comp, pl.ds(3, cells), pl.ds(row, ROWS), c].reshape(cells * ROWS, -1)
                    for c in (pl.ds(before, 128), cols, pl.ds(after, 128))
                ],
                axis=1,
            )
            flat[b, 2 * comp + 1] = jnp.dot(line, band_ref[...], preferred_element_type=F32)
        return s

    def depth_derivative(b, s, deep):
        row = pl.multiple_of(lax.rem(s + 1, tiles) * ROWS, ROWS)
        cols = pl.ds(pl.multiple_of(b * WIDE, WIDE), WIDE)
        for comp in range(3):
            column = vz[comp, :, pl.ds(row, ROWS), cols].reshape((cells + 6) * ROWS, WIDE)
            deep[comp] = jnp.dot(dz_ref[...], column, preferred_element_type=F32)

    def shade(b, s, deep):
        for h in range(WIDE // 128):
            to = b * (WIDE // 128) + h
            halves = []
            for r in range(ROWS // 8):
                cum = jnp.zeros((8, 128), F32)
                trans = jnp.ones((8, 128), F32)
                colour = [jnp.zeros((8, 128), F32) for _ in range(3)]
                for z in range(cells):
                    spot = (pl.ds(z * ROWS + 8 * r, 8), pl.ds(128 * h, 128))
                    a = [
                        [deep[j, spot[0], spot[1]]] + [flat[b, 2 * j + m, spot[0], spot[1]] for m in (0, 1)]
                        for j in range(3)
                    ]
                    q = a[0][0] * a[0][0] + a[1][1] * a[1][1] + a[2][2] * a[2][2]
                    q = q + 2.0 * (a[0][1] * a[1][0] + a[0][2] * a[2][0] + a[1][2] * a[2][1])
                    place = jnp.tanh(q * Q_SCALE) * (0.5 * (KNOTS - 1)) + 0.5 * (KNOTS - 1)
                    index = place.astype(jnp.int32)
                    part = (place - index.astype(F32)) * (HIGH / LOW)

                    def look(c, index=index, part=part):
                        entry = jnp.take_along_axis(tab[c], index, axis=1, mode="promise_in_bounds")
                        return entry.astype(F32) + (entry << 16).astype(F32) * part

                    cum = cum + look(3)
                    behind = jnp.exp2(cum * unit[3])
                    weight = trans - behind
                    trans = behind
                    colour = [colour[c] + look(c) * weight for c in range(3)]
                halves.append([colour[c] * unit[c] for c in range(3)] + [trans])
            for c in range(4):
                full = jnp.concatenate([half[c] for half in halves], axis=0)
                high = full.astype(BF)
                packets[s, to, c] = high
                if c == 3:
                    packets[s, to, 4] = (full - high.astype(F32)).astype(BF)

    def send(b, s):
        for h in range(WIDE // 128):
            to = b * (WIDE // 128) + h

            @pl.when(to == me)
            def _(to=to):
                a2a_own(s).start()

            @pl.when(to != me)
            def _(to=to):
                a2a_copy(s, to).start()

    def two_blocks(j, s):
        depth_derivative(2 * j + 1, s, deep_odd)
        shade(2 * j, s, deep_even)
        send(2 * j, s)
        depth_derivative(jnp.minimum(2 * j + 2, blocks - 1), s, deep_even)
        shade(2 * j + 1, s, deep_odd)
        send(2 * j + 1, s)
        return s

    def gather_copy(s, axis, i):
        return pltpu.make_async_remote_copy(
            src_ref=arrive.at[s, :, pl.ds(2 * axis, 2)],
            dst_ref=held.at[axis, s, pos[axis]],
            send_sem=s1_sem.at[s, axis, i - 1],
            recv_sem=r1_sem.at[s, axis, pos[axis]],
            device_id={"tile": peer(axis, i)[1]},
        )

    def gather_arrival(s, axis, i):
        place, to = peer(axis, i)
        return pltpu.make_async_remote_copy(
            src_ref=arrive.at[s, :, pl.ds(2 * axis, 2)],
            dst_ref=held.at[axis, s, place],
            send_sem=s1_sem.at[s, axis, i - 1],
            recv_sem=r1_sem.at[s, axis, place],
            device_id={"tile": to},
        )

    def pick_copy(s, axis, i):
        other = 1 - axis
        place, to = peer(other, i)
        return pltpu.make_async_remote_copy(
            src_ref=picked.at[axis, s, place],
            dst_ref=landed.at[axis, s, pos[other]],
            send_sem=s2_sem.at[s, axis, i - 1],
            recv_sem=r2_sem.at[s, axis, pos[other]],
            device_id={"tile": to},
        )

    def pick_arrival(s, axis, i):
        place, to = peer(1 - axis, i)
        return pltpu.make_async_remote_copy(
            src_ref=picked.at[axis, s, place],
            dst_ref=landed.at[axis, s, place],
            send_sem=s2_sem.at[s, axis, i - 1],
            recv_sem=r2_sem.at[s, axis, place],
            device_id={"tile": to},
        )

    def frame_step(s):
        rows = pl.ds(pl.multiple_of(lax.rem(s + 1, tiles) * ROWS, ROWS), ROWS)
        for i in range(1, n_depth):
            a2a_arrival(s, lax.rem(me + i, n_depth)).wait_recv()
        a2a_own(s).wait()
        for axis in (0, 1):
            for i in range(1, AXIS):
                gather_copy(s, axis, i).start()
        colour = [jnp.zeros((ROWS, 128), F32) for _ in range(3)]
        trans = jnp.ones((ROWS, 128), F32)
        for d in range(n_depth):
            image = [arrive[s, d, c] for c in range(5)]
            for axis in (0, 1):
                for c in (0, 1):
                    held[axis, s, pos[axis], d, c] = image[2 * axis + c]
            colour = [colour[c] + trans * image[c].astype(F32) for c in range(3)]
            trans = trans * (image[3].astype(F32) + image[4].astype(F32))
        for c in range(3):
            img_rgb[c, rows, :] = colour[c] + trans * colour[c]
        img_t[rows, :] = trans * trans

    def pick_step(s):
        @pl.when(s == 0)
        def _():
            for axis in (0, 1):
                for i in range(1, AXIS):
                    hot_arrival(axis, i).wait_recv()
            everything = pltpu.make_async_copy(hot_all, hot_here, hl_sem)
            everything.start()
            everything.wait()

        for axis in (0, 1):
            for i in range(1, AXIS):
                gather_arrival(s, axis, i).wait_recv()
            shelf[axis] = held[axis, s]
            for i in range(AXIS):
                place, _ = peer(1 - axis, i)
                for h in range(hot):
                    brick = hot_here[1 - axis, place, 0, h]
                    its_tile, slab = brick // n_depth, lax.rem(brick, n_depth)
                    its_place = its_tile // AXIS if axis == 0 else lax.rem(its_tile, AXIS)
                    image = shelf[axis, its_place, slab]
                    if i == 0:
                        landed[axis, s, place, h] = image
                    else:
                        picked[axis, s, place, h] = image
                if i > 0:
                    pick_copy(s, axis, i).start()

    def choose(axis, s, h, place):
        image = landed[axis, s, 0, h].astype(F32)
        for i in range(1, AXIS):
            image = jnp.where(place == i, landed[axis, s, i, h].astype(F32), image)
        return image

    def inset_step(s):
        rows = pl.ds(pl.multiple_of(lax.rem(s + 1, tiles) * ROWS, ROWS), ROWS)
        for axis in (0, 1):
            for i in range(1, AXIS):
                pick_arrival(s, axis, i).wait_recv()
        for h in range(hot):
            its_tile = hot_smem[0, h] // n_depth
            first = choose(0, s, h, lax.rem(its_tile, AXIS))
            last = choose(1, s, h, its_tile // AXIS)
            count = reps[0, h]
            trans = last[1]
            two = jnp.where(count >= 2, trans, 0.0)
            three = jnp.where(count >= 3, trans * trans, 0.0)
            total = 1.0 + two + three
            ins_rgb[0, h, 0, rows, :] = first[0] * total
            ins_rgb[0, h, 1, rows, :] = first[1] * total
            ins_rgb[0, h, 2, rows, :] = last[0] * total
            power = jnp.where(count >= 2, trans, 1.0) * trans
            ins_t[0, h, rows, :] = jnp.where(count >= 3, trans, 1.0) * power

    lax.fori_loop(0, blocks, first_second, 0)

    def step(k, carry):
        @pl.when(k < tiles)
        def _():
            z_copy(k, True).wait_recv()
            z_copy(k, False).wait_recv()
            depth_derivative(0, k, deep_even)
            lax.fori_loop(0, blocks // 2, two_blocks, k)

        @pl.when(k < tiles - 1)
        def _():
            for comp in range(3):

                @pl.when(k == tiles - 3)
                def _(comp=comp):
                    x_copy(0, comp).wait_recv()

                @pl.when(k == tiles - 2)
                def _(comp=comp):
                    x_copy(1, comp).wait_recv()

            lax.fori_loop(0, blocks, first_second, k + 1)

        @pl.when((k >= 1) & (k < tiles + 1))
        def _():
            frame_step(k - 1)

        @pl.when((k >= 2) & (k < tiles + 2))
        def _():
            pick_step(k - 2)

        @pl.when(k >= 3)
        def _():
            inset_step(k - 3)

        return carry

    lax.fori_loop(0, tiles + 3, step, 0)

    for axis in (0, 1):
        for i in range(1, AXIS):
            hot_copy(axis, i).wait_send()
    for comp in range(3):
        x_copy(0, comp).wait_send()
        x_copy(1, comp).wait_send()

    def sent(s, carry):
        z_copy(s, True).wait_send()
        z_copy(s, False).wait_send()
        for i in range(1, n_depth):
            a2a_copy(s, lax.rem(me + i, n_depth)).wait_send()
        for axis in (0, 1):
            for i in range(1, AXIS):
                gather_copy(s, axis, i).wait_send()
                pick_copy(s, axis, i).wait_send()
        return carry

    lax.fori_loop(0, tiles, sent, 0)


def body(velocity, palette, bin_table, hot_ids, repeats):
    _, cells, width, length = velocity.shape
    n_depth, n_tile = lax.axis_size("depth"), lax.axis_size("tile")
    hot = hot_ids.shape[1]
    tiles = width // ROWS
    groups = 3 * cells // 4
    vmem, hbm = pl.BlockSpec(memory_space=pltpu.VMEM), pl.BlockSpec(memory_space=pltpu.HBM)
    dma = pltpu.SemaphoreType.DMA
    constants = [
        jnp.asarray(m.astype(ml_dtypes.bfloat16))
        for m in (depth_matrix(cells), first_matrix(tiles), second_matrix(), pack_matrix())
    ]
    columns = length // n_depth
    operands = [
        pltpu.with_memory_space_constraint(x, pltpu.HBM)
        for x in (velocity, palette, bin_table, hot_ids, repeats, *constants)
    ]
    return pl.pallas_call(
        functools.partial(render_kernel, (cells, width, length, n_depth, n_tile, hot)),
        out_shape=(
            jax.ShapeDtypeStruct((3, width, columns), F32),
            jax.ShapeDtypeStruct((width, columns), F32),
            jax.ShapeDtypeStruct((1, hot, 3, width, columns), F32),
            jax.ShapeDtypeStruct((1, hot, width, columns), F32),
        ),
        in_specs=[hbm] * 9,
        out_specs=(vmem, vmem, vmem, vmem),
        scratch_shapes=[
            pltpu.SMEM(palette.shape, F32),
            pltpu.SMEM(bin_table.shape, jnp.int32),
            pltpu.SMEM(hot_ids.shape, jnp.int32),
            pltpu.VMEM(hot_ids.shape, jnp.int32),
            pltpu.SMEM(repeats.shape, jnp.int32),
            *[pltpu.VMEM(m.shape, BF) for m in constants],
            pltpu.VMEM((3, cells + 6, width, length), BF),
            pltpu.VMEM((2, groups, ROWS, length), BF),
            pltpu.VMEM((3, groups, ROWS, length), BF),
            pltpu.VMEM((length // WIDE, 6, cells * ROWS, WIDE), F32),
            pltpu.VMEM((3, cells * ROWS, WIDE), F32),
            pltpu.VMEM((3, cells * ROWS, WIDE), F32),
            pltpu.VMEM((4, 8, 128), jnp.int32),
            pltpu.VMEM((4, 8, 128), F32),
            pltpu.VMEM((tiles, n_depth, 5, ROWS, columns), BF),
            pltpu.VMEM((tiles, n_depth, 5, ROWS, columns), BF),
            pltpu.VMEM((2, tiles, AXIS, n_depth, 2, ROWS, columns), BF),
            pltpu.VMEM((2, AXIS, n_depth, 2, ROWS, columns), BF),
            pltpu.VMEM((2, tiles, AXIS, hot, 2, ROWS, columns), BF),
            pltpu.VMEM((2, tiles, AXIS, hot, 2, ROWS, columns), BF),
            pltpu.VMEM((2, AXIS, 1, hot), jnp.int32),
            pltpu.SMEM((2, AXIS, 1, hot), jnp.int32),
            dma((9,)), dma((tiles,)),
            dma((tiles, 2)), dma((tiles, 2)),
            dma((2, 3)), dma((2, 3)),
            dma((2, AXIS)), dma((2, AXIS)), pltpu.SemaphoreType.DMA,
            dma((tiles, n_depth)), dma((tiles, n_depth)),
            dma((tiles, 2, AXIS)), dma((tiles, 2, AXIS)),
            dma((tiles, 2, AXIS)), dma((tiles, 2, AXIS)),
        ],
        compiler_params=pltpu.CompilerParams(
            collective_id=0, has_side_effects=True, vmem_limit_bytes=48 * 2**20
        ),
        cost_estimate=pl.CostEstimate(
            flops=3 * cells * width * length * 400, bytes_accessed=velocity.size * 2, transcendentals=0
        ),
        name="render",
    )(*operands)


def solution(mesh):
    placed = (P(None, "depth", "tile", None), P(), P(), P("tile", None), P("tile", None))
    return jax.shard_map(
        body,
        mesh=mesh,
        in_specs=placed,
        out_specs=(
            P(None, "tile", "depth"),
            P("tile", "depth"),
            P("tile", None, None, None, "depth"),
            P("tile", None, None, "depth"),
        ),
        check_vma=False,
    )
```

```python
import functools
import math

import jax
import jax.numpy as jnp
import ml_dtypes
import numpy as np
from jax import lax
from jax.experimental import pallas as pl
from jax.experimental.pallas import tpu as pltpu
from jax.sharding import PartitionSpec as P

KNOTS = 17
MAXREP = 3
STENCIL = ((1, 45.0), (2, -9.0), (3, 1.0))
TAPS = tuple((k, c) for k, c in STENCIL) + tuple((-k, -c) for k, c in STENCIL)
HALF = 32760.0
Q_SCALE = -0.5 / 3600.0
BF = jnp.bfloat16
F32 = jnp.float32
ROWS = 16
WIDE = 256
AXIS = 4


def depth_matrix(cells):
    m = np.zeros((cells * ROWS, (cells + 6) * ROWS), np.float32)
    for z in range(cells):
        for r in range(ROWS):
            for k, c in TAPS:
                m[z * ROWS + r, (z + 3 + k) * ROWS + r] = c
    return m


def first_matrix(tiles):
    m = np.zeros((tiles, 4 * ROWS, 13 * ROWS), np.float32)
    for t in range(tiles):
        for p in range(4):
            for r in range(ROWS):
                for k, c in TAPS:
                    g = r + k
                    if 0 <= g < ROWS:
                        col = 4 * ROWS + p * ROWS + g
                    elif g < 0:
                        col = p * ROWS + ROWS + g if t > 0 else 12 * ROWS + 3 * p + 3 + g
                    else:
                        col = 8 * ROWS + p * ROWS + g - ROWS if t < tiles - 1 else 12 * ROWS + 3 * p + g - ROWS
                    m[t, p * ROWS + r, col] = c
    return m


def second_matrix():
    m = np.zeros((2 * WIDE, WIDE), np.float32)
    for l in range(WIDE):
        for k, c in TAPS:
            m[128 + l + k, l] = c
    return m


def pack_matrix():
    m = np.zeros((2, ROWS, 4 * ROWS), np.float32)
    for p in range(4):
        for r in range(3):
            m[0, 3 * p + r, p * ROWS + r] = 1.0
            m[1, 3 * p + r, p * ROWS + ROWS - 3 + r] = 1.0
    return m


def render_kernel(
    sizes,
    vel, palette_in, bins_in, hot_in, reps_in, dz_in, dx_in, band_in, pack_in,
    img_rgb, img_t, ins_rgb, ins_t,
    palette, bins, hot_smem, hot_vmem, reps, dz_ref, dx_ref, band_ref, pack_ref,
    vz, xsend, xh, flat_even, flat_odd, deep_even, deep_odd, tab, unit, packets, arrive, held, shelf, picked, landed, hot_all, hot_here,
    in_sem, own_sem, zs_sem, zr_sem, xs_sem, xr_sem, hs_sem, hr_sem, hl_sem,
    as_sem, ar_sem, s1_sem, r1_sem, s2_sem, r2_sem,
):
    cells, width, length, n_depth, n_tile, hot = sizes
    tiles = width // ROWS
    blocks = length // WIDE
    flats = (flat_even, flat_odd)
    tile = lax.axis_index("tile")
    me = lax.axis_index("depth")
    pos = (tile // AXIS, lax.rem(tile, AXIS))

    def peer(axis, i):
        place = lax.rem(pos[axis] + i, AXIS)
        return place, (place * AXIS + pos[1] if axis == 0 else pos[0] * AXIS + place)

    tile_up = lax.rem(tile + 1, n_tile)
    tile_down = lax.rem(tile + n_tile - 1, n_tile)
    depth_up = lax.rem(me + 1, n_depth)
    depth_down = lax.rem(me + n_depth - 1, n_depth)

    small = [
        pltpu.make_async_copy(source, target, in_sem.at[n])
        for n, (source, target) in enumerate(
            (
                (hot_in, hot_vmem), (pack_in, pack_ref), (palette_in, palette), (bins_in, bins),
                (hot_in, hot_smem), (reps_in, reps), (dz_in, dz_ref), (dx_in, dx_ref), (band_in, band_ref),
            )
        )
    ]

    def own_copy(t):
        rows = pl.ds(t * ROWS, ROWS)
        return pltpu.make_async_copy(
            vel.at[:, :, rows, :], vz.at[:, pl.ds(3, cells), rows, :], own_sem.at[t]
        )

    own_copy(0).start()
    own_copy(3).start()
    for copy in small:
        copy.start()
    own_copy(1).start()
    own_copy(2).start()

    barrier = pltpu.get_barrier_semaphore()
    for t in (tile_up, tile_down):
        pl.semaphore_signal(barrier, inc=1, device_id={"tile": t})
    for i in range(1, n_depth):
        pl.semaphore_signal(barrier, inc=1, device_id={"depth": lax.rem(me + i, n_depth)})
    for axis in (0, 1):
        for i in range(1, AXIS):
            pl.semaphore_signal(barrier, inc=1, device_id={"tile": peer(axis, i)[1]})
    pl.semaphore_wait(barrier, 2 + n_depth - 1 + 2 * (AXIS - 1))

    def z_copy(s, up):
        rows = pl.ds((s + 1) % tiles * ROWS, ROWS)
        source, target = (cells - 3, 0) if up else (0, cells + 3)
        return pltpu.make_async_remote_copy(
            src_ref=vel.at[:, pl.ds(source, 3), rows, :],
            dst_ref=vz.at[:, pl.ds(target, 3), rows, :],
            send_sem=zs_sem.at[s, int(up)],
            recv_sem=zr_sem.at[s, int(up)],
            device_id={"depth": depth_up if up else depth_down},
        )

    for s in range(3):
        for up in (True, False):
            z_copy(s, up).start()

    def hot_copy(axis, i):
        return pltpu.make_async_remote_copy(
            src_ref=hot_vmem,
            dst_ref=hot_all.at[axis, pos[axis]],
            send_sem=hs_sem.at[axis, i - 1],
            recv_sem=hr_sem.at[axis, pos[axis]],
            device_id={"tile": peer(axis, i)[1]},
        )

    def hot_arrival(axis, i):
        place, to = peer(axis, i)
        return pltpu.make_async_remote_copy(
            src_ref=hot_vmem, dst_ref=hot_all.at[axis, place],
            send_sem=hs_sem.at[axis, i - 1], recv_sem=hr_sem.at[axis, place],
            device_id={"tile": to},
        )

    small[0].wait()
    for axis in (0, 1):
        for i in range(1, AXIS):
            hot_copy(axis, i).start()
        hot_all[axis, pos[axis]] = hot_vmem[...]

    def x_copy(side, comp):
        groups = pl.ds(comp * (cells // 4), cells // 4)
        return pltpu.make_async_remote_copy(
            src_ref=xsend.at[side, groups],
            dst_ref=xh.at[1 - side, groups],
            send_sem=xs_sem.at[side, comp],
            recv_sem=xr_sem.at[side, comp],
            device_id={"tile": tile_up if side else tile_down},
        )

    own_copy(0).wait()
    own_copy(3).wait()
    small[1].wait()

    def pack(comp, carry):
        for side in (0, 1):
            rows = pl.ds((tiles - 1) * ROWS * side, ROWS)
            for quad in range(cells // 4):
                planes = vz[comp, pl.ds(3 + 4 * quad, 4), rows, :]
                xsend[side, comp * (cells // 4) + quad] = jnp.dot(
                    pack_ref[side], planes.reshape(4 * ROWS, length), preferred_element_type=F32
                ).astype(BF)
            x_copy(side, comp).start()
        return carry

    lax.fori_loop(0, 3, pack, 0)

    for copy in small[2:]:
        copy.wait()
    lane = lax.broadcasted_iota(jnp.int32, (8, 128), 1)
    for c in range(4):
        values = [palette[c, bins[k]] for k in range(KNOTS)]
        base = jnp.full((8, 128), values[KNOTS - 1], F32)
        following = base
        for k in range(KNOTS - 1):
            base = jnp.where(lane == k, values[k], base)
            following = jnp.where(lane == k, values[k + 1], following)
        top = jnp.broadcast_to(jnp.max(base, axis=1, keepdims=True), (8, 128))
        low = jnp.floor((following - base) / top * HALF + 0.5)
        high = jnp.floor(base / top * HALF - low * (1.0 / 65536.0) + 0.5)
        tab[c] = high.astype(jnp.int32) * 65536 + low.astype(jnp.int32)
        if c == 3:
            unit[c] = top * (-4.0 / (cells * n_depth) * math.log2(math.e) / (HALF * 65536.0))
        else:
            unit[c] = top * (1.0 / (HALF * 65536.0))

    own_copy(1).wait()
    own_copy(2).wait()

    def a2a_copy(s, to):
        return pltpu.make_async_remote_copy(
            src_ref=packets.at[s, to],
            dst_ref=arrive.at[s, me],
            send_sem=as_sem.at[s, to],
            recv_sem=ar_sem.at[s, me],
            device_id={"depth": to},
        )

    def a2a_arrival(s, source):
        return pltpu.make_async_remote_copy(
            src_ref=packets.at[s, source],
            dst_ref=arrive.at[s, source],
            send_sem=as_sem.at[s, source],
            recv_sem=ar_sem.at[s, source],
            device_id={"depth": source},
        )

    def a2a_own(s):
        return pltpu.make_async_copy(packets.at[s, me], arrive.at[s, me], ar_sem.at[s, me])

    def horizontal(b, s, first=True, second=True):
        t = (s + 1) % tiles
        flat = flats[s % 2]
        rows = [pl.ds(r * ROWS, ROWS) for r in (max(t - 1, 0), t, min(t + 1, tiles - 1))]
        side = {0: 0, tiles - 1: 1}.get(t)
        col = pl.multiple_of(b * WIDE, WIDE)
        before = pl.multiple_of(lax.rem(col + length - 128, length), 128)
        after = pl.multiple_of(lax.rem(col + WIDE, length), 128)
        cols = pl.ds(col, WIDE)
        for comp in range(3):
            for quad in range(cells // 4 if first else 0):
                zs = pl.ds(3 + 4 * quad, 4)
                parts = [vz[comp, zs, r, cols].reshape(4 * ROWS, WIDE) for r in rows]
                if side is not None:
                    parts.append(xh[side, comp * (cells // 4) + quad, :, cols])
                flat[b, 2 * comp, pl.ds(quad * 4 * ROWS, 4 * ROWS)] = jnp.dot(
                    dx_ref[t, :, : ROWS * (12 + (side is not None))],
                    jnp.concatenate(parts, axis=0),
                    preferred_element_type=F32,
                )
            if second:
                line = jnp.concatenate(
                    [
                        vz[comp, pl.ds(3, cells), rows[1], c].reshape(cells * ROWS, -1)
                        for c in (pl.ds(before, 128), cols, pl.ds(after, 128))
                    ],
                    axis=1,
                )
                flat[b, 2 * comp + 1] = jnp.dot(line, band_ref[...], preferred_element_type=F32)

    def horizontal_loop(s, first=True, second=True):
        def one(b, carry):
            horizontal(b, s, first, second)
            return carry

        lax.fori_loop(0, blocks, one, 0)

    def depth_derivative(b, s, deep):
        row = (s + 1) % tiles * ROWS
        cols = pl.ds(pl.multiple_of(b * WIDE, WIDE), WIDE)
        for comp in range(3):
            column = vz[comp, :, pl.ds(row, ROWS), cols].reshape((cells + 6) * ROWS, WIDE)
            deep[comp] = jnp.dot(dz_ref[...], column, preferred_element_type=F32)

    def shade(b, s, deep):
        flat = flats[s % 2]
        for h in range(WIDE // 128):
            to = b * (WIDE // 128) + h
            halves = []
            for r in range(ROWS // 8):
                cum = jnp.zeros((8, 128), F32)
                trans = jnp.ones((8, 128), F32)
                colour = [jnp.zeros((8, 128), F32) for _ in range(3)]
                for z in range(cells):
                    spot = (pl.ds(z * ROWS + 8 * r, 8), pl.ds(128 * h, 128))
                    a = [
                        [deep[j, spot[0], spot[1]]] + [flat[b, 2 * j + m, spot[0], spot[1]] for m in (0, 1)]
                        for j in range(3)
                    ]
                    q = a[0][0] * a[0][0] + a[1][1] * a[1][1] + a[2][2] * a[2][2]
                    q = q + 2.0 * (a[0][1] * a[1][0] + a[0][2] * a[2][0] + a[1][2] * a[2][1])
                    place = jnp.tanh(q * Q_SCALE) * (0.5 * (KNOTS - 1)) + 0.5 * (KNOTS - 1)
                    index = place.astype(jnp.int32)
                    part = place - index.astype(F32)

                    def look(c, index=index, part=part):
                        entry = jnp.take_along_axis(tab[c], index, axis=1, mode="promise_in_bounds")
                        return entry.astype(F32) + (entry << 16).astype(F32) * part

                    cum = cum + look(3)
                    behind = jnp.exp2(cum * unit[3])
                    weight = trans - behind
                    trans = behind
                    colour = [colour[c] + look(c) * weight for c in range(3)]
                halves.append([colour[c] * unit[c] for c in range(3)] + [trans])
            for c in range(4):
                full = jnp.concatenate([half[c] for half in halves], axis=0)
                high = full.astype(BF)
                packets[s, to, c] = high
                if c == 3:
                    packets[s, to, 4] = (full - high.astype(F32)).astype(BF)

    def send(b, s):
        for h in range(WIDE // 128):
            to = b * (WIDE // 128) + h

            @pl.when(to == me)
            def _(to=to):
                a2a_own(s).start()

            @pl.when(to != me)
            def _(to=to):
                a2a_copy(s, to).start()

    def chip_at(offset):
        return lax.rem(me // 2 + offset, blocks)

    def two_blocks(j, s, ahead):
        even, odd = chip_at(2 + j), chip_at(1 - j)
        depth_derivative(odd, s, deep_odd)
        ahead(2 * j)
        shade(even, s, deep_even)
        send(even, s)
        depth_derivative(chip_at(3), s, deep_even)
        ahead(2 * j + 1)
        shade(odd, s, deep_odd)
        send(odd, s)
        return s

    def render(s, ahead):
        def loop(j, carry):
            two_blocks(j, s, ahead)
            return carry

        z_copy(s, True).wait_recv()
        z_copy(s, False).wait_recv()
        depth_derivative(chip_at(2), s, deep_even)
        lax.fori_loop(0, blocks // 2, loop, 0)

    def gather_copy(s, axis, i):
        return pltpu.make_async_remote_copy(
            src_ref=arrive.at[s, :, pl.ds(2 * axis, 2)],
            dst_ref=held.at[axis, s, pos[axis]],
            send_sem=s1_sem.at[s, axis, i - 1],
            recv_sem=r1_sem.at[s, axis, pos[axis]],
            device_id={"tile": peer(axis, i)[1]},
        )

    def gather_arrival(s, axis, i):
        place, to = peer(axis, i)
        return pltpu.make_async_remote_copy(
            src_ref=arrive.at[s, :, pl.ds(2 * axis, 2)],
            dst_ref=held.at[axis, s, place],
            send_sem=s1_sem.at[s, axis, i - 1],
            recv_sem=r1_sem.at[s, axis, place],
            device_id={"tile": to},
        )

    def pick_copy(s, axis, i):
        other = 1 - axis
        place, to = peer(other, i)
        return pltpu.make_async_remote_copy(
            src_ref=picked.at[axis, s, place],
            dst_ref=landed.at[axis, s, pos[other]],
            send_sem=s2_sem.at[s, axis, i - 1],
            recv_sem=r2_sem.at[s, axis, pos[other]],
            device_id={"tile": to},
        )

    def pick_arrival(s, axis, i):
        place, to = peer(1 - axis, i)
        return pltpu.make_async_remote_copy(
            src_ref=picked.at[axis, s, place],
            dst_ref=landed.at[axis, s, place],
            send_sem=s2_sem.at[s, axis, i - 1],
            recv_sem=r2_sem.at[s, axis, place],
            device_id={"tile": to},
        )

    def frame_step(s):
        rows = pl.ds((s + 1) % tiles * ROWS, ROWS)
        for i in range(1, n_depth):
            a2a_arrival(s, lax.rem(me + i, n_depth)).wait_recv()
        a2a_own(s).wait()
        for axis in (0, 1):
            for i in range(1, AXIS):
                gather_copy(s, axis, i).start()
        colour = [jnp.zeros((ROWS, 128), F32) for _ in range(3)]
        trans = jnp.ones((ROWS, 128), F32)
        for d in range(n_depth):
            image = [arrive[s, d, c] for c in range(5)]
            for axis in (0, 1):
                for c in (0, 1):
                    held[axis, s, pos[axis], d, c] = image[2 * axis + c]
            colour = [colour[c] + trans * image[c].astype(F32) for c in range(3)]
            trans = trans * (image[3].astype(F32) + image[4].astype(F32))
        for c in range(3):
            img_rgb[c, rows, :] = colour[c] + trans * colour[c]
        img_t[rows, :] = trans * trans

    def pick_step(s):
        if s == 0:
            for axis in (0, 1):
                for i in range(1, AXIS):
                    hot_arrival(axis, i).wait_recv()
            everything = pltpu.make_async_copy(hot_all, hot_here, hl_sem)
            everything.start()
            everything.wait()

        for axis in (0, 1):
            for i in range(1, AXIS):
                gather_arrival(s, axis, i).wait_recv()
            shelf[axis] = held[axis, s]
            for i in range(AXIS):
                place, _ = peer(1 - axis, i)
                for h in range(hot):
                    brick = hot_here[1 - axis, place, 0, h]
                    its_tile, slab = brick // n_depth, lax.rem(brick, n_depth)
                    its_place = its_tile // AXIS if axis == 0 else lax.rem(its_tile, AXIS)
                    image = shelf[axis, its_place, slab]
                    if i == 0:
                        landed[axis, s, place, h] = image
                    else:
                        picked[axis, s, place, h] = image
                if i > 0:
                    pick_copy(s, axis, i).start()

    def choose(axis, s, h, place):
        image = landed[axis, s, 0, h].astype(F32)
        for i in range(1, AXIS):
            image = jnp.where(place == i, landed[axis, s, i, h].astype(F32), image)
        return image

    def inset_step(s):
        rows = pl.ds((s + 1) % tiles * ROWS, ROWS)
        for axis in (0, 1):
            for i in range(1, AXIS):
                pick_arrival(s, axis, i).wait_recv()
        for h in range(hot):
            its_tile = hot_smem[0, h] // n_depth
            first = choose(0, s, h, lax.rem(its_tile, AXIS))
            last = choose(1, s, h, its_tile // AXIS)
            count = reps[0, h]
            trans = last[1]
            two = jnp.where(count >= 2, trans, 0.0)
            three = jnp.where(count >= 3, trans * trans, 0.0)
            total = 1.0 + two + three
            ins_rgb[0, h, 0, rows, :] = first[0] * total
            ins_rgb[0, h, 1, rows, :] = first[1] * total
            ins_rgb[0, h, 2, rows, :] = last[0] * total
            power = jnp.where(count >= 2, trans, 1.0) * trans
            ins_t[0, h, rows, :] = jnp.where(count >= 3, trans, 1.0) * power

    def nothing(b):
        pass

    horizontal_loop(0)
    render(0, lambda b: horizontal(b, 1))
    for up in (True, False):
        z_copy(tiles - 1, up).start()
    render(1, lambda b: horizontal(b, 2, first=False))
    for comp in range(3):
        x_copy(0, comp).wait_recv()
    horizontal_loop(2, second=False)
    frame_step(0)
    for comp in range(3):
        x_copy(1, comp).wait_recv()
    render(2, lambda b: horizontal(b, 3))
    frame_step(1)
    pick_step(0)
    render(3, nothing)
    frame_step(2)
    pick_step(1)
    inset_step(0)
    frame_step(3)
    pick_step(2)
    inset_step(1)
    pick_step(3)
    inset_step(2)
    inset_step(3)

    for axis in (0, 1):
        for i in range(1, AXIS):
            hot_copy(axis, i).wait_send()
    for comp in range(3):
        x_copy(0, comp).wait_send()
        x_copy(1, comp).wait_send()

    def sent(s, carry):
        z_copy(s, True).wait_send()
        z_copy(s, False).wait_send()
        for i in range(1, n_depth):
            a2a_copy(s, lax.rem(me + i, n_depth)).wait_send()
        for axis in (0, 1):
            for i in range(1, AXIS):
                gather_copy(s, axis, i).wait_send()
                pick_copy(s, axis, i).wait_send()
        return carry

    lax.fori_loop(0, tiles, sent, 0)


def body(velocity, palette, bin_table, hot_ids, repeats):
    _, cells, width, length = velocity.shape
    n_depth, n_tile = lax.axis_size("depth"), lax.axis_size("tile")
    hot = hot_ids.shape[1]
    tiles = width // ROWS
    groups = 3 * cells // 4
    vmem, hbm = pl.BlockSpec(memory_space=pltpu.VMEM), pl.BlockSpec(memory_space=pltpu.HBM)
    dma = pltpu.SemaphoreType.DMA
    constants = [
        jnp.asarray(m.astype(ml_dtypes.bfloat16))
        for m in (depth_matrix(cells), first_matrix(tiles), second_matrix(), pack_matrix())
    ]
    columns = length // n_depth
    operands = [
        pltpu.with_memory_space_constraint(x, pltpu.HBM)
        for x in (velocity, palette, bin_table, hot_ids, repeats, *constants)
    ]
    return pl.pallas_call(
        functools.partial(render_kernel, (cells, width, length, n_depth, n_tile, hot)),
        out_shape=(
            jax.ShapeDtypeStruct((3, width, columns), F32),
            jax.ShapeDtypeStruct((width, columns), F32),
            jax.ShapeDtypeStruct((1, hot, 3, width, columns), F32),
            jax.ShapeDtypeStruct((1, hot, width, columns), F32),
        ),
        in_specs=[hbm] * 9,
        out_specs=(vmem, vmem, vmem, vmem),
        scratch_shapes=[
            pltpu.SMEM(palette.shape, F32),
            pltpu.SMEM(bin_table.shape, jnp.int32),
            pltpu.SMEM(hot_ids.shape, jnp.int32),
            pltpu.VMEM(hot_ids.shape, jnp.int32),
            pltpu.SMEM(repeats.shape, jnp.int32),
            *[pltpu.VMEM(m.shape, BF) for m in constants],
            pltpu.VMEM((3, cells + 6, width, length), BF),
            pltpu.VMEM((2, groups, ROWS, length), BF),
            pltpu.VMEM((2, groups, ROWS, length), BF),
            pltpu.VMEM((length // WIDE, 6, cells * ROWS, WIDE), F32),
            pltpu.VMEM((length // WIDE, 6, cells * ROWS, WIDE), F32),
            pltpu.VMEM((3, cells * ROWS, WIDE), F32),
            pltpu.VMEM((3, cells * ROWS, WIDE), F32),
            pltpu.VMEM((4, 8, 128), jnp.int32),
            pltpu.VMEM((4, 8, 128), F32),
            pltpu.VMEM((tiles, n_depth, 5, ROWS, columns), BF),
            pltpu.VMEM((tiles, n_depth, 5, ROWS, columns), BF),
            pltpu.VMEM((2, tiles, AXIS, n_depth, 2, ROWS, columns), BF),
            pltpu.VMEM((2, AXIS, n_depth, 2, ROWS, columns), BF),
            pltpu.VMEM((2, tiles, AXIS, hot, 2, ROWS, columns), BF),
            pltpu.VMEM((2, tiles, AXIS, hot, 2, ROWS, columns), BF),
            pltpu.VMEM((2, AXIS, 1, hot), jnp.int32),
            pltpu.SMEM((2, AXIS, 1, hot), jnp.int32),
            dma((9,)), dma((tiles,)),
            dma((tiles, 2)), dma((tiles, 2)),
            dma((2, 3)), dma((2, 3)),
            dma((2, AXIS)), dma((2, AXIS)), pltpu.SemaphoreType.DMA,
            dma((tiles, n_depth)), dma((tiles, n_depth)),
            dma((tiles, 2, AXIS)), dma((tiles, 2, AXIS)),
            dma((tiles, 2, AXIS)), dma((tiles, 2, AXIS)),
        ],
        compiler_params=pltpu.CompilerParams(
            collective_id=0, has_side_effects=True, vmem_limit_bytes=48 * 2**20
        ),
        cost_estimate=pl.CostEstimate(
            flops=3 * cells * width * length * 400, bytes_accessed=velocity.size * 2, transcendentals=0
        ),
        name="render",
    )(*operands)


def solution(mesh):
    placed = (P(None, "depth", "tile", None), P(), P(), P("tile", None), P("tile", None))
    return jax.shard_map(
        body,
        mesh=mesh,
        in_specs=placed,
        out_specs=(
            P(None, "tile", "depth"),
            P("tile", "depth"),
            P("tile", None, None, None, "depth"),
            P("tile", None, None, "depth"),
        ),
        check_vma=False,
    )
```

```python
import functools
import math

import jax
import jax.numpy as jnp
import ml_dtypes
import numpy as np
from jax import lax
from jax.experimental import pallas as pl
from jax.experimental.pallas import tpu as pltpu
from jax.sharding import PartitionSpec as P

KNOTS = 17
MAXREP = 3
STENCIL = ((1, 45.0), (2, -9.0), (3, 1.0))
TAPS = tuple((k, c) for k, c in STENCIL) + tuple((-k, -c) for k, c in STENCIL)
HALF = 32760.0
Q_SCALE = -0.5 / 3600.0
BF = jnp.bfloat16
F32 = jnp.float32
ROWS = 16
WIDE = 256
AXIS = 4


def depth_matrix(cells):
    m = np.zeros((cells * ROWS, (cells + 6) * ROWS), np.float32)
    for z in range(cells):
        for r in range(ROWS):
            for k, c in TAPS:
                m[z * ROWS + r, (z + 3 + k) * ROWS + r] = c
    return m


def first_matrices(cells):
    inner = np.zeros((4 * ROWS, 12 * ROWS), np.float32)
    edge = np.zeros((2, cells // 4, 4 * ROWS, 8 * ROWS + 3 * cells), np.float32)
    for p in range(4):
        for r in range(ROWS):
            for k, c in TAPS:
                g, row = r + k, p * ROWS + r
                part = 1 + (g >= ROWS) - (g < 0)
                spot = p * ROWS + g % ROWS
                inner[row, part * 4 * ROWS + spot] = c
                for quad in range(cells // 4):
                    packed = 8 * ROWS + 3 * (4 * quad + p)
                    edge[0, quad, row, packed + 3 + g if g < 0 else (part - 1) * 4 * ROWS + spot] = c
                    edge[1, quad, row, packed + g - ROWS if g >= ROWS else part * 4 * ROWS + spot] = c
    return inner, edge


def second_matrix():
    m = np.zeros((2 * WIDE, WIDE), np.float32)
    for l in range(WIDE):
        for k, c in TAPS:
            m[128 + l + k, l] = c
    return m


def pack_matrix(cells):
    m = np.zeros((2, 3 * cells, cells * ROWS), np.float32)
    for p in range(cells):
        for r in range(3):
            m[0, 3 * p + r, p * ROWS + r] = 1.0
            m[1, 3 * p + r, p * ROWS + ROWS - 3 + r] = 1.0
    return m


def render_kernel(
    sizes,
    vel, palette_in, bins_in, hot_in, reps_in, dz_in, inner_in, edge_in, band_in, pack_in,
    img_rgb, img_t, ins_rgb, ins_t,
    palette, bins, hot_smem, hot_vmem, reps, dz_ref, inner_ref, edge_ref, band_ref, pack_ref,
    vz, xsend, xh, flat_even, flat_odd, deep_even, deep_odd, tab, unit, packets, arrive, held, shelf, picked, landed, hot_all, hot_here,
    in_sem, own_sem, zs_sem, zr_sem, xs_sem, xr_sem, hs_sem, hr_sem, hl_sem,
    as_sem, ar_sem, s1_sem, r1_sem, s2_sem, r2_sem,
):
    cells, width, length, n_depth, n_tile, hot = sizes
    tiles = width // ROWS
    blocks = length // WIDE
    flats = (flat_even, flat_odd)
    tile = lax.axis_index("tile")
    me = lax.axis_index("depth")
    pos = (tile // AXIS, lax.rem(tile, AXIS))

    def peer(axis, i):
        place = lax.rem(pos[axis] + i, AXIS)
        return place, (place * AXIS + pos[1] if axis == 0 else pos[0] * AXIS + place)

    tile_up = lax.rem(tile + 1, n_tile)
    tile_down = lax.rem(tile + n_tile - 1, n_tile)
    depth_up = lax.rem(me + 1, n_depth)
    depth_down = lax.rem(me + n_depth - 1, n_depth)

    small = [
        pltpu.make_async_copy(source, target, in_sem.at[n])
        for n, (source, target) in enumerate(
            (
                (hot_in, hot_vmem), (pack_in, pack_ref), (palette_in, palette), (bins_in, bins),
                (hot_in, hot_smem), (reps_in, reps), (dz_in, dz_ref), (inner_in, inner_ref), (edge_in, edge_ref), (band_in, band_ref),
            )
        )
    ]

    def own_copy(t):
        rows = pl.ds(t * ROWS, ROWS)
        return pltpu.make_async_copy(
            vel.at[:, :, rows, :], vz.at[:, pl.ds(3, cells), rows, :], own_sem.at[t]
        )

    own_copy(0).start()
    own_copy(3).start()
    for copy in small:
        copy.start()
    own_copy(1).start()
    own_copy(2).start()

    barrier = pltpu.get_barrier_semaphore()
    for t in (tile_up, tile_down):
        pl.semaphore_signal(barrier, inc=1, device_id={"tile": t})
    for i in range(1, n_depth):
        pl.semaphore_signal(barrier, inc=1, device_id={"depth": lax.rem(me + i, n_depth)})
    for axis in (0, 1):
        for i in range(1, AXIS):
            pl.semaphore_signal(barrier, inc=1, device_id={"tile": peer(axis, i)[1]})
    pl.semaphore_wait(barrier, 2 + n_depth - 1 + 2 * (AXIS - 1))

    def z_copy(s, up):
        rows = pl.ds((s + 1) % tiles * ROWS, ROWS)
        source, target = (cells - 3, 0) if up else (0, cells + 3)
        return pltpu.make_async_remote_copy(
            src_ref=vel.at[:, pl.ds(source, 3), rows, :],
            dst_ref=vz.at[:, pl.ds(target, 3), rows, :],
            send_sem=zs_sem.at[s, int(up)],
            recv_sem=zr_sem.at[s, int(up)],
            device_id={"depth": depth_up if up else depth_down},
        )

    for s in range(3):
        for up in (True, False):
            z_copy(s, up).start()

    def hot_copy(axis, i):
        return pltpu.make_async_remote_copy(
            src_ref=hot_vmem,
            dst_ref=hot_all.at[axis, pos[axis]],
            send_sem=hs_sem.at[axis, i - 1],
            recv_sem=hr_sem.at[axis, pos[axis]],
            device_id={"tile": peer(axis, i)[1]},
        )

    def hot_arrival(axis, i):
        place, to = peer(axis, i)
        return pltpu.make_async_remote_copy(
            src_ref=hot_vmem, dst_ref=hot_all.at[axis, place],
            send_sem=hs_sem.at[axis, i - 1], recv_sem=hr_sem.at[axis, place],
            device_id={"tile": to},
        )

    small[0].wait()
    for axis in (0, 1):
        for i in range(1, AXIS):
            hot_copy(axis, i).start()
        hot_all[axis, pos[axis]] = hot_vmem[...]

    def x_copy(side, comp):
        return pltpu.make_async_remote_copy(
            src_ref=xsend.at[side, comp],
            dst_ref=xh.at[1 - side, comp],
            send_sem=xs_sem.at[side, comp],
            recv_sem=xr_sem.at[side, comp],
            device_id={"tile": tile_up if side else tile_down},
        )

    own_copy(0).wait()
    own_copy(3).wait()
    small[1].wait()

    def pack(comp, carry):
        for side in (0, 1):
            rows = pl.ds((tiles - 1) * ROWS * side, ROWS)
            planes = vz[comp, pl.ds(3, cells), rows, :].reshape(cells * ROWS, length)
            xsend[side, comp] = jnp.dot(pack_ref[side], planes, preferred_element_type=F32).astype(BF)
            x_copy(side, comp).start()
        return carry

    lax.fori_loop(0, 3, pack, 0)

    for copy in small[2:]:
        copy.wait()
    lane = lax.broadcasted_iota(jnp.int32, (8, 128), 1)
    for c in range(4):
        values = [palette[c, bins[k]] for k in range(KNOTS)]
        base = jnp.full((8, 128), values[KNOTS - 1], F32)
        following = base
        for k in range(KNOTS - 1):
            base = jnp.where(lane == k, values[k], base)
            following = jnp.where(lane == k, values[k + 1], following)
        top = jnp.broadcast_to(jnp.max(base, axis=1, keepdims=True), (8, 128))
        low = jnp.floor((following - base) / top * HALF + 0.5)
        high = jnp.floor(base / top * HALF - low * (1.0 / 65536.0) + 0.5)
        tab[c] = high.astype(jnp.int32) * 65536 + low.astype(jnp.int32)
        if c == 3:
            unit[c] = top * (-4.0 / (cells * n_depth) * math.log2(math.e) / (HALF * 65536.0))
        else:
            unit[c] = top * (1.0 / (HALF * 65536.0))

    own_copy(1).wait()
    own_copy(2).wait()

    def a2a_copy(s, to):
        return pltpu.make_async_remote_copy(
            src_ref=packets.at[s, to],
            dst_ref=arrive.at[s, me],
            send_sem=as_sem.at[s, to],
            recv_sem=ar_sem.at[s, me],
            device_id={"depth": to},
        )

    def a2a_arrival(s, source):
        return pltpu.make_async_remote_copy(
            src_ref=packets.at[s, source],
            dst_ref=arrive.at[s, source],
            send_sem=as_sem.at[s, source],
            recv_sem=ar_sem.at[s, source],
            device_id={"depth": source},
        )

    def a2a_own(s):
        return pltpu.make_async_copy(packets.at[s, me], arrive.at[s, me], ar_sem.at[s, me])

    def horizontal(b, s):
        t = (s + 1) % tiles
        flat = flats[s % 2]
        own = pl.ds(t * ROWS, ROWS)
        side = {0: 0, tiles - 1: 1}.get(t)
        rows = [pl.ds(r * ROWS, ROWS) for r in (t - 1, t, t + 1) if 0 <= r < tiles]
        col = pl.multiple_of(b * WIDE, WIDE)
        before = pl.multiple_of(lax.rem(col + length - 128, length), 128)
        after = pl.multiple_of(lax.rem(col + WIDE, length), 128)
        cols = pl.ds(col, WIDE)
        for comp in range(3):
            for quad in range(cells // 4):
                zs = pl.ds(3 + 4 * quad, 4)
                parts = [vz[comp, zs, r, cols].reshape(4 * ROWS, WIDE) for r in rows]
                if side is not None:
                    parts.append(xh[side, comp, :, cols])
                flat[b, 2 * comp, pl.ds(quad * 4 * ROWS, 4 * ROWS)] = jnp.dot(
                    inner_ref[...] if side is None else edge_ref[side, quad],
                    jnp.concatenate(parts, axis=0),
                    preferred_element_type=F32,
                )
            line = jnp.concatenate(
                [
                    vz[comp, pl.ds(3, cells), own, c].reshape(cells * ROWS, -1)
                    for c in (pl.ds(before, 128), cols, pl.ds(after, 128))
                ],
                axis=1,
            )
            flat[b, 2 * comp + 1] = jnp.dot(line, band_ref[...], preferred_element_type=F32)

    def horizontal_loop(s):
        def one(b, carry):
            horizontal(b, s)
            return carry

        lax.fori_loop(0, blocks, one, 0)

    def depth_derivative(b, s, deep):
        size = cells // 2 * ROWS
        row = (s + 1) % tiles * ROWS
        cols = pl.ds(pl.multiple_of(b * WIDE, WIDE), WIDE)
        for comp in range(3):
            column = vz[comp, :, pl.ds(row, ROWS), cols].reshape((cells + 6) * ROWS, WIDE)
            for half in (0, 1):
                window = column[half * size : half * size + (cells // 2 + 6) * ROWS]
                deep[comp, pl.ds(half * size, size)] = jnp.dot(
                    dz_ref[...], window, preferred_element_type=F32
                )

    def shade(b, s, deep):
        flat = flats[s % 2]
        for h in range(WIDE // 128):
            to = b * (WIDE // 128) + h
            halves = []
            for r in range(ROWS // 8):
                cum = jnp.zeros((8, 128), F32)
                trans = jnp.ones((8, 128), F32)
                colour = [jnp.zeros((8, 128), F32) for _ in range(3)]
                for z in range(cells):
                    spot = (pl.ds(z * ROWS + 8 * r, 8), pl.ds(128 * h, 128))
                    a = [
                        [deep[j, spot[0], spot[1]]] + [flat[b, 2 * j + m, spot[0], spot[1]] for m in (0, 1)]
                        for j in range(3)
                    ]
                    q = a[0][0] * a[0][0] + a[1][1] * a[1][1] + a[2][2] * a[2][2]
                    q = q + 2.0 * (a[0][1] * a[1][0] + a[0][2] * a[2][0] + a[1][2] * a[2][1])
                    place = jnp.tanh(q * Q_SCALE) * (0.5 * (KNOTS - 1)) + 0.5 * (KNOTS - 1)
                    index = place.astype(jnp.int32)
                    part = place - index.astype(F32)

                    def look(c, index=index, part=part):
                        entry = jnp.take_along_axis(tab[c], index, axis=1, mode="promise_in_bounds")
                        return entry.astype(F32) + (entry << 16).astype(F32) * part

                    cum = cum + look(3)
                    behind = jnp.exp2(cum * unit[3])
                    weight = trans - behind
                    trans = behind
                    colour = [colour[c] + look(c) * weight for c in range(3)]
                halves.append([colour[c] * unit[c] for c in range(3)] + [trans])
            for c in range(4):
                full = jnp.concatenate([half[c] for half in halves], axis=0)
                high = full.astype(BF)
                packets[s, to, c] = high
                if c == 3:
                    packets[s, to, 4] = (full - high.astype(F32)).astype(BF)

    def send(b, s):
        for h in range(WIDE // 128):
            to = b * (WIDE // 128) + h

            @pl.when(to == me)
            def _(to=to):
                a2a_own(s).start()

            @pl.when(to != me)
            def _(to=to):
                a2a_copy(s, to).start()

    def chip_at(offset):
        return lax.rem(me // 2 + offset, blocks)

    def two_blocks(j, s, ahead):
        even, odd = chip_at(2 + j), chip_at(1 - j)
        depth_derivative(odd, s, deep_odd)
        ahead(2 * j)
        shade(even, s, deep_even)
        send(even, s)
        depth_derivative(chip_at(3), s, deep_even)
        ahead(2 * j + 1)
        shade(odd, s, deep_odd)
        send(odd, s)
        return s

    def render(s, ahead):
        def loop(j, carry):
            two_blocks(j, s, ahead)
            return carry

        z_copy(s, True).wait_recv()
        z_copy(s, False).wait_recv()
        depth_derivative(chip_at(2), s, deep_even)
        lax.fori_loop(0, blocks // 2, loop, 0)

    def gather_copy(s, axis, i):
        return pltpu.make_async_remote_copy(
            src_ref=arrive.at[s, :, pl.ds(2 * axis, 2)],
            dst_ref=held.at[axis, s, pos[axis]],
            send_sem=s1_sem.at[s, axis, i - 1],
            recv_sem=r1_sem.at[s, axis, pos[axis]],
            device_id={"tile": peer(axis, i)[1]},
        )

    def gather_arrival(s, axis, i):
        place, to = peer(axis, i)
        return pltpu.make_async_remote_copy(
            src_ref=arrive.at[s, :, pl.ds(2 * axis, 2)],
            dst_ref=held.at[axis, s, place],
            send_sem=s1_sem.at[s, axis, i - 1],
            recv_sem=r1_sem.at[s, axis, place],
            device_id={"tile": to},
        )

    def pick_copy(s, axis, i):
        other = 1 - axis
        place, to = peer(other, i)
        return pltpu.make_async_remote_copy(
            src_ref=picked.at[axis, s, place],
            dst_ref=landed.at[axis, s, pos[other]],
            send_sem=s2_sem.at[s, axis, i - 1],
            recv_sem=r2_sem.at[s, axis, pos[other]],
            device_id={"tile": to},
        )

    def pick_arrival(s, axis, i):
        place, to = peer(1 - axis, i)
        return pltpu.make_async_remote_copy(
            src_ref=picked.at[axis, s, place],
            dst_ref=landed.at[axis, s, place],
            send_sem=s2_sem.at[s, axis, i - 1],
            recv_sem=r2_sem.at[s, axis, place],
            device_id={"tile": to},
        )

    def frame_step(s):
        rows = pl.ds((s + 1) % tiles * ROWS, ROWS)
        for i in range(1, n_depth):
            a2a_arrival(s, lax.rem(me + i, n_depth)).wait_recv()
        a2a_own(s).wait()
        for axis in (0, 1):
            for i in range(1, AXIS):
                gather_copy(s, axis, i).start()
        colour = [jnp.zeros((ROWS, 128), F32) for _ in range(3)]
        trans = jnp.ones((ROWS, 128), F32)
        for d in range(n_depth):
            image = [arrive[s, d, c] for c in range(5)]
            for axis in (0, 1):
                for c in (0, 1):
                    held[axis, s, pos[axis], d, c] = image[2 * axis + c]
            colour = [colour[c] + trans * image[c].astype(F32) for c in range(3)]
            trans = trans * (image[3].astype(F32) + image[4].astype(F32))
        for c in range(3):
            img_rgb[c, rows, :] = colour[c] + trans * colour[c]
        img_t[rows, :] = trans * trans

    def pick_step(s):
        if s == 0:
            for axis in (0, 1):
                for i in range(1, AXIS):
                    hot_arrival(axis, i).wait_recv()
            everything = pltpu.make_async_copy(hot_all, hot_here, hl_sem)
            everything.start()
            everything.wait()

        for axis in (0, 1):
            for i in range(1, AXIS):
                gather_arrival(s, axis, i).wait_recv()
            shelf[axis] = held[axis, s]
            for i in range(AXIS):
                place, _ = peer(1 - axis, i)
                for h in range(hot):
                    brick = hot_here[1 - axis, place, 0, h]
                    its_tile, slab = brick // n_depth, lax.rem(brick, n_depth)
                    its_place = its_tile // AXIS if axis == 0 else lax.rem(its_tile, AXIS)
                    image = shelf[axis, its_place, slab]
                    if i == 0:
                        landed[axis, s, place, h] = image
                    else:
                        picked[axis, s, place, h] = image
                if i > 0:
                    pick_copy(s, axis, i).start()

    def choose(axis, s, h, place):
        image = landed[axis, s, 0, h].astype(F32)
        for i in range(1, AXIS):
            image = jnp.where(place == i, landed[axis, s, i, h].astype(F32), image)
        return image

    def inset_step(s):
        rows = pl.ds((s + 1) % tiles * ROWS, ROWS)
        for axis in (0, 1):
            for i in range(1, AXIS):
                pick_arrival(s, axis, i).wait_recv()
        for h in range(hot):
            its_tile = hot_smem[0, h] // n_depth
            first = choose(0, s, h, lax.rem(its_tile, AXIS))
            last = choose(1, s, h, its_tile // AXIS)
            count = reps[0, h]
            trans = last[1]
            two = jnp.where(count >= 2, trans, 0.0)
            three = jnp.where(count >= 3, trans * trans, 0.0)
            total = 1.0 + two + three
            ins_rgb[0, h, 0, rows, :] = first[0] * total
            ins_rgb[0, h, 1, rows, :] = first[1] * total
            ins_rgb[0, h, 2, rows, :] = last[0] * total
            power = jnp.where(count >= 2, trans, 1.0) * trans
            ins_t[0, h, rows, :] = jnp.where(count >= 3, trans, 1.0) * power

    def nothing(b):
        pass

    horizontal_loop(0)
    render(0, lambda b: horizontal(b, 1))
    for up in (True, False):
        z_copy(tiles - 1, up).start()
    for comp in range(3):
        x_copy(0, comp).wait_recv()
    render(1, lambda b: horizontal(b, 2))
    frame_step(0)
    for comp in range(3):
        x_copy(1, comp).wait_recv()
    render(2, lambda b: horizontal(b, 3))
    frame_step(1)
    pick_step(0)
    render(3, nothing)
    frame_step(2)
    pick_step(1)
    inset_step(0)
    frame_step(3)
    pick_step(2)
    inset_step(1)
    pick_step(3)
    inset_step(2)
    inset_step(3)

    for axis in (0, 1):
        for i in range(1, AXIS):
            hot_copy(axis, i).wait_send()
    for comp in range(3):
        x_copy(0, comp).wait_send()
        x_copy(1, comp).wait_send()

    def sent(s, carry):
        z_copy(s, True).wait_send()
        z_copy(s, False).wait_send()
        for i in range(1, n_depth):
            a2a_copy(s, lax.rem(me + i, n_depth)).wait_send()
        for axis in (0, 1):
            for i in range(1, AXIS):
                gather_copy(s, axis, i).wait_send()
                pick_copy(s, axis, i).wait_send()
        return carry

    lax.fori_loop(0, tiles, sent, 0)


def body(velocity, palette, bin_table, hot_ids, repeats):
    _, cells, width, length = velocity.shape
    n_depth, n_tile = lax.axis_size("depth"), lax.axis_size("tile")
    hot = hot_ids.shape[1]
    tiles = width // ROWS
    vmem, hbm = pl.BlockSpec(memory_space=pltpu.VMEM), pl.BlockSpec(memory_space=pltpu.HBM)
    dma = pltpu.SemaphoreType.DMA
    constants = [
        jnp.asarray(m.astype(ml_dtypes.bfloat16))
        for m in (depth_matrix(cells // 2), *first_matrices(cells), second_matrix(), pack_matrix(cells))
    ]
    columns = length // n_depth
    operands = [
        pltpu.with_memory_space_constraint(x, pltpu.HBM)
        for x in (velocity, palette, bin_table, hot_ids, repeats, *constants)
    ]
    return pl.pallas_call(
        functools.partial(render_kernel, (cells, width, length, n_depth, n_tile, hot)),
        out_shape=(
            jax.ShapeDtypeStruct((3, width, columns), F32),
            jax.ShapeDtypeStruct((width, columns), F32),
            jax.ShapeDtypeStruct((1, hot, 3, width, columns), F32),
            jax.ShapeDtypeStruct((1, hot, width, columns), F32),
        ),
        in_specs=[hbm] * 10,
        out_specs=(vmem, vmem, vmem, vmem),
        scratch_shapes=[
            pltpu.SMEM(palette.shape, F32),
            pltpu.SMEM(bin_table.shape, jnp.int32),
            pltpu.SMEM(hot_ids.shape, jnp.int32),
            pltpu.VMEM(hot_ids.shape, jnp.int32),
            pltpu.SMEM(repeats.shape, jnp.int32),
            *[pltpu.VMEM(m.shape, BF) for m in constants],
            pltpu.VMEM((3, cells + 6, width, length), BF),
            pltpu.VMEM((2, 3, 3 * cells, length), BF),
            pltpu.VMEM((2, 3, 3 * cells, length), BF),
            pltpu.VMEM((length // WIDE, 6, cells * ROWS, WIDE), F32),
            pltpu.VMEM((length // WIDE, 6, cells * ROWS, WIDE), F32),
            pltpu.VMEM((3, cells * ROWS, WIDE), F32),
            pltpu.VMEM((3, cells * ROWS, WIDE), F32),
            pltpu.VMEM((4, 8, 128), jnp.int32),
            pltpu.VMEM((4, 8, 128), F32),
            pltpu.VMEM((tiles, n_depth, 5, ROWS, columns), BF),
            pltpu.VMEM((tiles, n_depth, 5, ROWS, columns), BF),
            pltpu.VMEM((2, tiles, AXIS, n_depth, 2, ROWS, columns), BF),
            pltpu.VMEM((2, AXIS, n_depth, 2, ROWS, columns), BF),
            pltpu.VMEM((2, tiles, AXIS, hot, 2, ROWS, columns), BF),
            pltpu.VMEM((2, tiles, AXIS, hot, 2, ROWS, columns), BF),
            pltpu.VMEM((2, AXIS, 1, hot), jnp.int32),
            pltpu.SMEM((2, AXIS, 1, hot), jnp.int32),
            dma((10,)), dma((tiles,)),
            dma((tiles, 2)), dma((tiles, 2)),
            dma((2, 3)), dma((2, 3)),
            dma((2, AXIS)), dma((2, AXIS)), pltpu.SemaphoreType.DMA,
            dma((tiles, n_depth)), dma((tiles, n_depth)),
            dma((tiles, 2, AXIS)), dma((tiles, 2, AXIS)),
            dma((tiles, 2, AXIS)), dma((tiles, 2, AXIS)),
        ],
        compiler_params=pltpu.CompilerParams(
            collective_id=0, has_side_effects=True, vmem_limit_bytes=48 * 2**20
        ),
        cost_estimate=pl.CostEstimate(
            flops=3 * cells * width * length * 400, bytes_accessed=velocity.size * 2, transcendentals=0
        ),
        name="render",
    )(*operands)


def solution(mesh):
    placed = (P(None, "depth", "tile", None), P(), P(), P("tile", None), P("tile", None))
    return jax.shard_map(
        body,
        mesh=mesh,
        in_specs=placed,
        out_specs=(
            P(None, "tile", "depth"),
            P("tile", "depth"),
            P("tile", None, None, None, "depth"),
            P("tile", None, None, "depth"),
        ),
        check_vma=False,
    )
```

```python
import functools
import math

import jax
import jax.numpy as jnp
import ml_dtypes
import numpy as np
from jax import lax
from jax.experimental import pallas as pl
from jax.experimental.pallas import tpu as pltpu
from jax.sharding import PartitionSpec as P

KNOTS = 17
MAXREP = 3
STENCIL = ((1, 45.0), (2, -9.0), (3, 1.0))
TAPS = tuple((k, c) for k, c in STENCIL) + tuple((-k, -c) for k, c in STENCIL)
HALF = 32760.0
Q_SCALE = -0.5 / 3600.0
BF = jnp.bfloat16
F32 = jnp.float32
ROWS = 16
WIDE = 256
AXIS = 4


def depth_matrix(cells):
    m = np.zeros((cells * ROWS, (cells + 6) * ROWS), np.float32)
    for z in range(cells):
        for r in range(ROWS):
            for k, c in TAPS:
                m[z * ROWS + r, (z + 3 + k) * ROWS + r] = c
    return m


def first_matrices(cells):
    inner = np.zeros((4 * ROWS, 12 * ROWS), np.float32)
    edge = np.zeros((2, cells // 4, 4 * ROWS, 8 * ROWS + 3 * cells), np.float32)
    for p in range(4):
        for r in range(ROWS):
            for k, c in TAPS:
                g, row = r + k, p * ROWS + r
                part = 1 + (g >= ROWS) - (g < 0)
                spot = p * ROWS + g % ROWS
                inner[row, part * 4 * ROWS + spot] = c
                for quad in range(cells // 4):
                    packed = 8 * ROWS + 3 * (4 * quad + p)
                    edge[0, quad, row, packed + 3 + g if g < 0 else (part - 1) * 4 * ROWS + spot] = c
                    edge[1, quad, row, packed + g - ROWS if g >= ROWS else part * 4 * ROWS + spot] = c
    return inner, edge


def second_matrix():
    m = np.zeros((2 * WIDE, WIDE), np.float32)
    for l in range(WIDE):
        for k, c in TAPS:
            m[128 + l + k, l] = c
    return m


def pack_matrix(cells):
    m = np.zeros((2, 3 * cells, cells * ROWS), np.float32)
    for p in range(cells):
        for r in range(3):
            m[0, 3 * p + r, p * ROWS + r] = 1.0
            m[1, 3 * p + r, p * ROWS + ROWS - 3 + r] = 1.0
    return m


def render_kernel(
    sizes,
    vel, palette_in, bins_in, hot_in, reps_in, dz_in, inner_in, edge_in, band_in, pack_in,
    img_rgb, img_t, ins_rgb, ins_t,
    palette, bins, hot_smem, hot_vmem, reps, dz_ref, inner_ref, edge_ref, band_ref, pack_ref,
    vz, xsend, xh, flat_even, flat_odd, deep_even, deep_odd, tab, unit, packets, arrive, held, shelf, picked, landed, hot_all, hot_here,
    in_sem, own_sem, zs_sem, zr_sem, xs_sem, xr_sem, hs_sem, hr_sem, hl_sem,
    as_sem, ar_sem, s1_sem, r1_sem, s2_sem, r2_sem,
):
    cells, width, length, n_depth, n_tile, hot = sizes
    tiles = width // ROWS
    blocks = length // WIDE
    flats = (flat_even, flat_odd)
    tile = lax.axis_index("tile")
    me = lax.axis_index("depth")
    pos = (tile // AXIS, lax.rem(tile, AXIS))

    def peer(axis, i):
        place = lax.rem(pos[axis] + i, AXIS)
        return place, (place * AXIS + pos[1] if axis == 0 else pos[0] * AXIS + place)

    tile_up = lax.rem(tile + 1, n_tile)
    tile_down = lax.rem(tile + n_tile - 1, n_tile)
    depth_up = lax.rem(me + 1, n_depth)
    depth_down = lax.rem(me + n_depth - 1, n_depth)

    small = [
        pltpu.make_async_copy(source, target, in_sem.at[n])
        for n, (source, target) in enumerate(
            (
                (hot_in, hot_vmem), (pack_in, pack_ref), (palette_in, palette), (bins_in, bins),
                (hot_in, hot_smem), (reps_in, reps), (dz_in, dz_ref), (inner_in, inner_ref), (edge_in, edge_ref), (band_in, band_ref),
            )
        )
    ]

    def own_copy(t):
        rows = pl.ds(t * ROWS, ROWS)
        return pltpu.make_async_copy(
            vel.at[:, :, rows, :], vz.at[:, pl.ds(3, cells), rows, :], own_sem.at[t]
        )

    own_copy(0).start()
    own_copy(3).start()
    for copy in small:
        copy.start()
    own_copy(1).start()
    own_copy(2).start()

    barrier = pltpu.get_barrier_semaphore()
    for t in (tile_up, tile_down):
        pl.semaphore_signal(barrier, inc=1, device_id={"tile": t})
    for i in range(1, n_depth):
        pl.semaphore_signal(barrier, inc=1, device_id={"depth": lax.rem(me + i, n_depth)})
    for axis in (0, 1):
        for i in range(1, AXIS):
            pl.semaphore_signal(barrier, inc=1, device_id={"tile": peer(axis, i)[1]})
    pl.semaphore_wait(barrier, 2 + n_depth - 1 + 2 * (AXIS - 1))

    def z_copy(s, up):
        rows = pl.ds((s + 1) % tiles * ROWS, ROWS)
        source, target = (cells - 3, 0) if up else (0, cells + 3)
        return pltpu.make_async_remote_copy(
            src_ref=vel.at[:, pl.ds(source, 3), rows, :],
            dst_ref=vz.at[:, pl.ds(target, 3), rows, :],
            send_sem=zs_sem.at[s, int(up)],
            recv_sem=zr_sem.at[s, int(up)],
            device_id={"depth": depth_up if up else depth_down},
        )

    for s in range(3):
        for up in (True, False):
            z_copy(s, up).start()

    def hot_copy(axis, i):
        return pltpu.make_async_remote_copy(
            src_ref=hot_vmem,
            dst_ref=hot_all.at[axis, pos[axis]],
            send_sem=hs_sem.at[axis, i - 1],
            recv_sem=hr_sem.at[axis, pos[axis]],
            device_id={"tile": peer(axis, i)[1]},
        )

    def hot_arrival(axis, i):
        place, to = peer(axis, i)
        return pltpu.make_async_remote_copy(
            src_ref=hot_vmem, dst_ref=hot_all.at[axis, place],
            send_sem=hs_sem.at[axis, i - 1], recv_sem=hr_sem.at[axis, place],
            device_id={"tile": to},
        )

    small[0].wait()
    for axis in (0, 1):
        for i in range(1, AXIS):
            hot_copy(axis, i).start()
        hot_all[axis, pos[axis]] = hot_vmem[...]

    def x_copy(side, comp):
        return pltpu.make_async_remote_copy(
            src_ref=xsend.at[side, comp],
            dst_ref=xh.at[1 - side, comp],
            send_sem=xs_sem.at[side, comp],
            recv_sem=xr_sem.at[side, comp],
            device_id={"tile": tile_up if side else tile_down},
        )

    own_copy(0).wait()
    own_copy(3).wait()
    small[1].wait()

    def pack(comp, carry):
        for side in (0, 1):
            rows = pl.ds((tiles - 1) * ROWS * side, ROWS)
            planes = vz[comp, pl.ds(3, cells), rows, :].reshape(cells * ROWS, length)
            xsend[side, comp] = jnp.dot(pack_ref[side], planes, preferred_element_type=F32).astype(BF)
            x_copy(side, comp).start()
        return carry

    lax.fori_loop(0, 3, pack, 0)

    for copy in small[2:]:
        copy.wait()
    lane = lax.broadcasted_iota(jnp.int32, (8, 128), 1)
    for c in range(4):
        values = [palette[c, bins[k]] for k in range(KNOTS)]
        base = jnp.full((8, 128), values[KNOTS - 1], F32)
        following = base
        for k in range(KNOTS - 1):
            base = jnp.where(lane == k, values[k], base)
            following = jnp.where(lane == k, values[k + 1], following)
        top = jnp.broadcast_to(jnp.max(base, axis=1, keepdims=True), (8, 128))
        low = jnp.floor((following - base) / top * HALF + 0.5)
        high = jnp.floor(base / top * HALF - low * (1.0 / 65536.0) + 0.5)
        tab[c] = high.astype(jnp.int32) * 65536 + low.astype(jnp.int32)
        if c == 3:
            unit[c] = top * (-4.0 / (cells * n_depth) * math.log2(math.e) / (HALF * 65536.0))
        else:
            unit[c] = top * (1.0 / (HALF * 65536.0))

    own_copy(1).wait()
    own_copy(2).wait()

    def a2a_copy(s, to):
        return pltpu.make_async_remote_copy(
            src_ref=packets.at[s, to],
            dst_ref=arrive.at[s, me],
            send_sem=as_sem.at[s, to],
            recv_sem=ar_sem.at[s, me],
            device_id={"depth": to},
        )

    def a2a_arrival(s, source):
        return pltpu.make_async_remote_copy(
            src_ref=packets.at[s, source],
            dst_ref=arrive.at[s, source],
            send_sem=as_sem.at[s, source],
            recv_sem=ar_sem.at[s, source],
            device_id={"depth": source},
        )

    def a2a_own(s):
        return pltpu.make_async_copy(packets.at[s, me], arrive.at[s, me], ar_sem.at[s, me])

    def horizontal(b, s):
        t = (s + 1) % tiles
        flat = flats[s % 2]
        own = pl.ds(t * ROWS, ROWS)
        side = {0: 0, tiles - 1: 1}.get(t)
        rows = [pl.ds(r * ROWS, ROWS) for r in (t - 1, t, t + 1) if 0 <= r < tiles]
        col = pl.multiple_of(b * WIDE, WIDE)
        before = pl.multiple_of(lax.rem(col + length - 128, length), 128)
        after = pl.multiple_of(lax.rem(col + WIDE, length), 128)
        cols = pl.ds(col, WIDE)
        for comp in range(3):
            for quad in range(cells // 4):
                zs = pl.ds(3 + 4 * quad, 4)
                parts = [vz[comp, zs, r, cols].reshape(4 * ROWS, WIDE) for r in rows]
                if side is not None:
                    parts.append(xh[side, comp, :, cols])
                flat[b, 2 * comp, pl.ds(quad * 4 * ROWS, 4 * ROWS)] = jnp.dot(
                    inner_ref[...] if side is None else edge_ref[side, quad],
                    jnp.concatenate(parts, axis=0),
                    preferred_element_type=F32,
                )
            line = jnp.concatenate(
                [
                    vz[comp, pl.ds(3, cells), own, c].reshape(cells * ROWS, -1)
                    for c in (pl.ds(before, 128), cols, pl.ds(after, 128))
                ],
                axis=1,
            )
            flat[b, 2 * comp + 1] = jnp.dot(line, band_ref[...], preferred_element_type=F32)

    def horizontal_loop(s):
        def one(b, carry):
            horizontal(b, s)
            return carry

        lax.fori_loop(0, blocks, one, 0)

    def depth_derivative(b, s, deep):
        size = cells // 2 * ROWS
        row = (s + 1) % tiles * ROWS
        cols = pl.ds(pl.multiple_of(b * WIDE, WIDE), WIDE)
        for comp in range(3):
            column = vz[comp, :, pl.ds(row, ROWS), cols].reshape((cells + 6) * ROWS, WIDE)
            for half in (0, 1):
                window = column[half * size : half * size + (cells // 2 + 6) * ROWS]
                deep[comp, pl.ds(half * size, size)] = jnp.dot(
                    dz_ref[...], window, preferred_element_type=F32
                )

    def shade(b, s, deep):
        flat = flats[s % 2]
        for h in range(WIDE // 128):
            to = b * (WIDE // 128) + h
            halves = []
            for r in range(ROWS // 8):
                cum = jnp.zeros((8, 128), F32)
                trans = jnp.ones((8, 128), F32)
                colour = [jnp.zeros((8, 128), F32) for _ in range(3)]
                for z in range(cells):
                    spot = (pl.ds(z * ROWS + 8 * r, 8), pl.ds(128 * h, 128))
                    a = [
                        [deep[j, spot[0], spot[1]]] + [flat[b, 2 * j + m, spot[0], spot[1]] for m in (0, 1)]
                        for j in range(3)
                    ]
                    q = a[0][0] * a[0][0] + a[1][1] * a[1][1] + a[2][2] * a[2][2]
                    q = q + 2.0 * (a[0][1] * a[1][0] + a[0][2] * a[2][0] + a[1][2] * a[2][1])
                    place = jnp.tanh(q * Q_SCALE) * (0.5 * (KNOTS - 1)) + 0.5 * (KNOTS - 1)
                    index = place.astype(jnp.int32)
                    part = place - index.astype(F32)

                    def look(c, index=index, part=part):
                        entry = jnp.take_along_axis(tab[c], index, axis=1, mode="promise_in_bounds")
                        return entry.astype(F32) + (entry << 16).astype(F32) * part

                    cum = cum + look(3)
                    behind = jnp.exp2(cum * unit[3])
                    weight = trans - behind
                    trans = behind
                    colour = [colour[c] + look(c) * weight for c in range(3)]
                halves.append([colour[c] * unit[c] for c in range(3)] + [trans])
            for c in range(4):
                full = jnp.concatenate([half[c] for half in halves], axis=0)
                high = full.astype(BF)
                packets[s, to, c] = high
                if c == 3:
                    packets[s, to, 4] = (full - high.astype(F32)).astype(BF)

    def send(b, s):
        for h in range(WIDE // 128):
            to = b * (WIDE // 128) + h

            @pl.when(to == me)
            def _(to=to):
                a2a_own(s).start()

            @pl.when(to != me)
            def _(to=to):
                a2a_copy(s, to).start()

    def chip_at(offset):
        return lax.rem(me // 2 + offset, blocks)

    def two_blocks(j, s, ahead):
        even, odd = chip_at(2 + j), chip_at(1 - j)
        depth_derivative(odd, s, deep_odd)
        ahead(2 * j)
        shade(even, s, deep_even)
        send(even, s)
        depth_derivative(chip_at(3), s, deep_even)
        ahead(2 * j + 1)
        shade(odd, s, deep_odd)
        send(odd, s)
        return s

    def render(s, ahead):
        def loop(j, carry):
            two_blocks(j, s, ahead)
            return carry

        z_copy(s, True).wait_recv()
        z_copy(s, False).wait_recv()
        depth_derivative(chip_at(2), s, deep_even)
        lax.fori_loop(0, blocks // 2, loop, 0)

    def gather_copy(s, axis, i):
        return pltpu.make_async_remote_copy(
            src_ref=arrive.at[s, :, pl.ds(2 * axis, 2)],
            dst_ref=held.at[axis, s, pos[axis]],
            send_sem=s1_sem.at[s, axis, i - 1],
            recv_sem=r1_sem.at[s, axis, pos[axis]],
            device_id={"tile": peer(axis, i)[1]},
        )

    def gather_arrival(s, axis, i):
        place, to = peer(axis, i)
        return pltpu.make_async_remote_copy(
            src_ref=arrive.at[s, :, pl.ds(2 * axis, 2)],
            dst_ref=held.at[axis, s, place],
            send_sem=s1_sem.at[s, axis, i - 1],
            recv_sem=r1_sem.at[s, axis, place],
            device_id={"tile": to},
        )

    def pick_copy(s, axis, i):
        other = 1 - axis
        place, to = peer(other, i)
        return pltpu.make_async_remote_copy(
            src_ref=picked.at[axis, s, place],
            dst_ref=landed.at[axis, s, pos[other]],
            send_sem=s2_sem.at[s, axis, i - 1],
            recv_sem=r2_sem.at[s, axis, pos[other]],
            device_id={"tile": to},
        )

    def pick_arrival(s, axis, i):
        place, to = peer(1 - axis, i)
        return pltpu.make_async_remote_copy(
            src_ref=picked.at[axis, s, place],
            dst_ref=landed.at[axis, s, place],
            send_sem=s2_sem.at[s, axis, i - 1],
            recv_sem=r2_sem.at[s, axis, place],
            device_id={"tile": to},
        )

    def frame_step(s):
        rows = pl.ds((s + 1) % tiles * ROWS, ROWS)
        for i in range(1, n_depth):
            a2a_arrival(s, lax.rem(me + i, n_depth)).wait_recv()
        a2a_own(s).wait()
        for axis in (0, 1):
            for i in range(1, AXIS):
                gather_copy(s, axis, i).start()
        colour = [jnp.zeros((ROWS, 128), F32) for _ in range(3)]
        trans = jnp.ones((ROWS, 128), F32)
        for d in range(n_depth):
            image = [arrive[s, d, c] for c in range(5)]
            for axis in (0, 1):
                for c in (0, 1):
                    held[axis, s, pos[axis], d, c] = image[2 * axis + c]
            colour = [colour[c] + trans * image[c].astype(F32) for c in range(3)]
            trans = trans * (image[3].astype(F32) + image[4].astype(F32))
        for c in range(3):
            img_rgb[c, rows, :] = colour[c] + trans * colour[c]
        img_t[rows, :] = trans * trans

    def pick_step(s):
        if s == 0:
            for axis in (0, 1):
                for i in range(1, AXIS):
                    hot_arrival(axis, i).wait_recv()
            everything = pltpu.make_async_copy(hot_all, hot_here, hl_sem)
            everything.start()
            everything.wait()

        for axis in (0, 1):
            for i in range(1, AXIS):
                gather_arrival(s, axis, i).wait_recv()
            shelf[axis] = held[axis, s]
            for i in (1, 2, 3, 0):
                place, _ = peer(1 - axis, i)
                for h in range(hot):
                    brick = hot_here[1 - axis, place, 0, h]
                    its_tile, slab = lax.div(brick, n_depth), lax.rem(brick, n_depth)
                    its_place = lax.div(its_tile, AXIS) if axis == 0 else lax.rem(its_tile, AXIS)
                    image = shelf[axis, its_place, slab]
                    if i == 0:
                        landed[axis, s, place, h] = image
                    else:
                        picked[axis, s, place, h] = image
                if i > 0:
                    pick_copy(s, axis, i).start()

    def choose(axis, s, h, place):
        image = landed[axis, s, 0, h].astype(F32)
        for i in range(1, AXIS):
            image = jnp.where(place == i, landed[axis, s, i, h].astype(F32), image)
        return image

    def inset_step(s):
        rows = pl.ds((s + 1) % tiles * ROWS, ROWS)
        for axis in (0, 1):
            for i in range(1, AXIS):
                pick_arrival(s, axis, i).wait_recv()
        for h in range(hot):
            its_tile = hot_smem[0, h] // n_depth
            first = choose(0, s, h, lax.rem(its_tile, AXIS))
            last = choose(1, s, h, its_tile // AXIS)
            count = reps[0, h]
            trans = last[1]
            two = jnp.where(count >= 2, trans, 0.0)
            three = jnp.where(count >= 3, trans * trans, 0.0)
            total = 1.0 + two + three
            ins_rgb[0, h, 0, rows, :] = first[0] * total
            ins_rgb[0, h, 1, rows, :] = first[1] * total
            ins_rgb[0, h, 2, rows, :] = last[0] * total
            power = jnp.where(count >= 2, trans, 1.0) * trans
            ins_t[0, h, rows, :] = jnp.where(count >= 3, trans, 1.0) * power

    def nothing(b):
        pass

    horizontal_loop(0)
    render(0, lambda b: horizontal(b, 1))
    for up in (True, False):
        z_copy(tiles - 1, up).start()
    for comp in range(3):
        x_copy(0, comp).wait_recv()
    render(1, lambda b: horizontal(b, 2))
    frame_step(0)
    for comp in range(3):
        x_copy(1, comp).wait_recv()
    render(2, lambda b: horizontal(b, 3))
    frame_step(1)
    pick_step(0)
    render(3, nothing)
    frame_step(2)
    pick_step(1)
    inset_step(0)
    frame_step(3)
    pick_step(2)
    inset_step(1)

    for axis in (0, 1):
        for i in range(1, AXIS):
            hot_copy(axis, i).wait_send()
    for comp in range(3):
        x_copy(0, comp).wait_send()
        x_copy(1, comp).wait_send()

    def images_sent(s, carry):
        z_copy(s, True).wait_send()
        z_copy(s, False).wait_send()
        for i in range(1, n_depth):
            a2a_copy(s, lax.rem(me + i, n_depth)).wait_send()
        return carry

    def bricks_sent(s, carry):
        for axis in (0, 1):
            for i in range(1, AXIS):
                gather_copy(s, axis, i).wait_send()
                pick_copy(s, axis, i).wait_send()
        return carry

    lax.fori_loop(0, tiles, images_sent, 0)
    lax.fori_loop(0, tiles - 2, bricks_sent, 0)
    pick_step(3)
    inset_step(2)
    bricks_sent(tiles - 2, 0)
    inset_step(3)
    bricks_sent(tiles - 1, 0)


def body(velocity, palette, bin_table, hot_ids, repeats):
    _, cells, width, length = velocity.shape
    n_depth, n_tile = lax.axis_size("depth"), lax.axis_size("tile")
    hot = hot_ids.shape[1]
    tiles = width // ROWS
    vmem, hbm = pl.BlockSpec(memory_space=pltpu.VMEM), pl.BlockSpec(memory_space=pltpu.HBM)
    dma = pltpu.SemaphoreType.DMA
    constants = [
        jnp.asarray(m.astype(ml_dtypes.bfloat16))
        for m in (depth_matrix(cells // 2), *first_matrices(cells), second_matrix(), pack_matrix(cells))
    ]
    columns = length // n_depth
    operands = [
        pltpu.with_memory_space_constraint(x, pltpu.HBM)
        for x in (velocity, palette, bin_table, hot_ids, repeats, *constants)
    ]
    return pl.pallas_call(
        functools.partial(render_kernel, (cells, width, length, n_depth, n_tile, hot)),
        out_shape=(
            jax.ShapeDtypeStruct((3, width, columns), F32),
            jax.ShapeDtypeStruct((width, columns), F32),
            jax.ShapeDtypeStruct((1, hot, 3, width, columns), F32),
            jax.ShapeDtypeStruct((1, hot, width, columns), F32),
        ),
        in_specs=[hbm] * 10,
        out_specs=(vmem, vmem, vmem, vmem),
        scratch_shapes=[
            pltpu.SMEM(palette.shape, F32),
            pltpu.SMEM(bin_table.shape, jnp.int32),
            pltpu.SMEM(hot_ids.shape, jnp.int32),
            pltpu.VMEM(hot_ids.shape, jnp.int32),
            pltpu.SMEM(repeats.shape, jnp.int32),
            *[pltpu.VMEM(m.shape, BF) for m in constants],
            pltpu.VMEM((3, cells + 6, width, length), BF),
            pltpu.VMEM((2, 3, 3 * cells, length), BF),
            pltpu.VMEM((2, 3, 3 * cells, length), BF),
            pltpu.VMEM((length // WIDE, 6, cells * ROWS, WIDE), F32),
            pltpu.VMEM((length // WIDE, 6, cells * ROWS, WIDE), F32),
            pltpu.VMEM((3, cells * ROWS, WIDE), F32),
            pltpu.VMEM((3, cells * ROWS, WIDE), F32),
            pltpu.VMEM((4, 8, 128), jnp.int32),
            pltpu.VMEM((4, 8, 128), F32),
            pltpu.VMEM((tiles, n_depth, 5, ROWS, columns), BF),
            pltpu.VMEM((tiles, n_depth, 5, ROWS, columns), BF),
            pltpu.VMEM((2, tiles, AXIS, n_depth, 2, ROWS, columns), BF),
            pltpu.VMEM((2, AXIS, n_depth, 2, ROWS, columns), BF),
            pltpu.VMEM((2, tiles, AXIS, hot, 2, ROWS, columns), BF),
            pltpu.VMEM((2, tiles, AXIS, hot, 2, ROWS, columns), BF),
            pltpu.VMEM((2, AXIS, 1, hot), jnp.int32),
            pltpu.SMEM((2, AXIS, 1, hot), jnp.int32),
            dma((10,)), dma((tiles,)),
            dma((tiles, 2)), dma((tiles, 2)),
            dma((2, 3)), dma((2, 3)),
            dma((2, AXIS)), dma((2, AXIS)), pltpu.SemaphoreType.DMA,
            dma((tiles, n_depth)), dma((tiles, n_depth)),
            dma((tiles, 2, AXIS)), dma((tiles, 2, AXIS)),
            dma((tiles, 2, AXIS)), dma((tiles, 2, AXIS)),
        ],
        compiler_params=pltpu.CompilerParams(
            collective_id=0, has_side_effects=True, vmem_limit_bytes=48 * 2**20
        ),
        cost_estimate=pl.CostEstimate(
            flops=3 * cells * width * length * 400, bytes_accessed=velocity.size * 2, transcendentals=0
        ),
        name="render",
    )(*operands)


def solution(mesh):
    placed = (P(None, "depth", "tile", None), P(), P(), P("tile", None), P("tile", None))
    return jax.shard_map(
        body,
        mesh=mesh,
        in_specs=placed,
        out_specs=(
            P(None, "tile", "depth"),
            P("tile", "depth"),
            P("tile", None, None, None, "depth"),
            P("tile", None, None, "depth"),
        ),
        check_vma=False,
    )
```
